128 devices in a mesh: dp: 8 (over z, y_hi), ctx: 16 (over x, y_lo, core).
Axes of the slice: x: 4, y: 4 (y_hi: 2, y_lo: 2; y = y_hi * 2 + y_lo), z: 4, core: 2. Of those that a mesh axis runs over, the one named last changes fastest.
Arguments:
- inputs: bfloat16 [8, 4096, 1536], P('dp', 'ctx'), may hold values from -6 to 6
- block_ids: int32 [8, 32], P('dp'), may hold values from 0 to 2, never falling along the last dimension, each value on 1 to 24 neighbouring positions
- attn_gain: float32 [1536], replicated, may hold values from 0.1 to 1.9
- w_qkv: bfloat16 [1536, 2304], replicated, may hold values from -6 to 6
- w_out: bfloat16 [768, 1536], replicated, may hold values from -0.21875 to 0.21875
- conv_gain: float32 [1536], replicated, may hold values from 0.1 to 1.9
- conv_in: bfloat16 [1536, 3072], P(None, 'dp'), may hold values from -0.15625 to 0.15625
- depthwise_w: float32 [31, 1536], replicated, may hold values from -1 to 1
- depth_gain: float32 [1536], replicated, may hold values from 0.1 to 1.9
- conv_out: bfloat16 [1536, 1536], replicated, may hold values from -0.15625 to 0.15625
Outputs:
- output: bfloat16 [8, 4096, 1536], P('dp', 'ctx')
The draws below stay inside these ranges and needn't reach their ends.
Inputs may be any that keep to these rules, and one draw needn't show every extreme that they name: `block_ids`: utterance numbers never fall along a row; a row holds 3 utterances of 1 to 24 blocks, one of exactly 24 blocks.
All inputs are finite; a program needn't handle non-finite values.
Results may differ from the reference program's by a relative error of at most 0.01.
Values may be sent and summed in bfloat16 or wider, within the bound.
A program may use at most 192 MiB of HBM per device.

```python
import math
import jax
import jax.numpy as jnp
import numpy as np
from jax import lax

MODEL_DIM = 1536
HEAD_COUNT = 8
HEAD_DIM = 96
KERNEL = 31
BLOCK_LEN = 128
UTTERANCES = 3
ROW_COUNT = 8
FRAMES = 4096
BLOCK_COUNT = 32
MOST_BLOCKS = 24


def draw_w_qkv(key, part):
    key = jax.random.fold_in(key, 11)
    query_seed, key_seed, value_seed = jax.random.split(key, 3)
    columns = HEAD_COUNT * HEAD_DIM
    score_spread = 1.6 / math.sqrt(MODEL_DIM)
    query_columns = jax.random.normal(query_seed, (MODEL_DIM, columns), jnp.float32) * score_spread
    value_columns = jax.random.normal(value_seed, (MODEL_DIM, columns), jnp.float32) / math.sqrt(MODEL_DIM)
    key_columns = jax.random.normal(key_seed, (MODEL_DIM, columns), jnp.float32) * score_spread
    return jnp.concatenate([query_columns, key_columns, value_columns], axis=1).astype(jnp.bfloat16)


def level_of(own_key, dims, cuts, least, top_value):
    def one(dim, parts):
        draws = jax.random.uniform(jax.random.fold_in(jax.random.fold_in(own_key, 6), dim), (parts,), jnp.float32, least / len(cuts), top_value / len(cuts))
        return jnp.repeat(jnp.exp(draws), dims[dim] // parts).reshape((-1,) + (1,) * (len(dims) - dim - 1))

    level = one(*cuts[0])
    for cut in cuts[1:]:
        level = level * one(*cut)
    return level


def split_up(count, total, reach, lean):
    loads = [(1 << 20) // math.isqrt(grade ** lean) + 1 for grade in range(2, count + 1)]
    surplus, counts = total - reach - (count - 1), [1] * (count - 1)
    while surplus > 0:
        movable = [i for i in range(count - 1) if counts[i] < reach]
        mass, budget = sum([loads[i] for i in movable]), surplus
        for i in movable:
            extra = min(reach - counts[i], max(1, budget * loads[i] // mass), surplus)
            counts[i] = counts[i] + extra
            surplus = surplus - extra
    return np.array([reach] + counts)


def uneven(stream_key, count, total, limit, slope):
    if count == 2:
        one = jax.random.randint(stream_key, (), max(1, total - limit), min(limit, total - 1) + 1)
        return jnp.stack([one, total - one])
    lengths = jnp.asarray(split_up(count, total, limit, slope), jnp.int32)
    couples = (count - 1) // 2
    giver, sink = lengths[1:1 + 2 * couples:2], lengths[2:2 + 2 * couples:2]
    margin = jnp.minimum(giver - 1, limit - sink)
    shifted = jax.random.randint(jax.random.fold_in(stream_key, 1), (couples,), 0, 1 << 20) % (margin + 1)
    lengths = lengths.at[1:1 + 2 * couples:2].set(giver - shifted).at[2:2 + 2 * couples:2].set(sink + shifted)
    return lengths[jax.random.permutation(jax.random.fold_in(stream_key, 2), count)]


def normal_values(own_key, dims, width, limit, cuts=(), kind=jnp.bfloat16):
    gain = level_of(own_key, dims, cuts, -0.22, 0.18) if cuts else 1.0
    entries = jax.random.normal(own_key, dims, jnp.float32) * width * gain
    return jnp.minimum(jnp.maximum(entries, -limit), limit).astype(kind)


def setup_inputs(seed: int = 0) -> dict:
    seeds = jax.random.split(jax.random.key(seed), 11)
    inputs = normal_values(seeds[0], (ROW_COUNT, FRAMES, MODEL_DIM), 1.0, 6.0, ((0, 8), (1, 16)))
    block_ids = jax.vmap(lambda own: jnp.searchsorted(jnp.cumsum(uneven(own, UTTERANCES, BLOCK_COUNT, MOST_BLOCKS, 0)), jnp.arange(BLOCK_COUNT), side="right"))(jax.random.split(seeds[1], ROW_COUNT)).reshape((ROW_COUNT, BLOCK_COUNT)).astype(jnp.int32)
    attn_gain = jnp.clip(1.0 + 0.18 * jax.random.normal(seeds[2], (MODEL_DIM,), jnp.float32), 0.1, 1.9)
    w_qkv = draw_w_qkv(jax.random.fold_in(seeds[10], 71), 0)
    w_out = normal_values(seeds[4], (HEAD_COUNT * HEAD_DIM, MODEL_DIM), (HEAD_COUNT * HEAD_DIM) ** -0.5, 0.21875)
    conv_gain = jnp.clip(1.0 + 0.18 * jax.random.normal(seeds[5], (MODEL_DIM,), jnp.float32), 0.1, 1.9)
    conv_in = normal_values(seeds[6], (MODEL_DIM, 2 * MODEL_DIM), MODEL_DIM ** -0.5, 0.15625, ((1, 8),))
    depthwise_w = normal_values(seeds[7], (KERNEL, MODEL_DIM), KERNEL ** -0.5, 1.0, (), jnp.float32)
    depth_gain = jnp.clip(1.0 + 0.18 * jax.random.normal(seeds[8], (MODEL_DIM,), jnp.float32), 0.1, 1.9)
    conv_out = normal_values(seeds[9], (MODEL_DIM, MODEL_DIM), MODEL_DIM ** -0.5, 0.15625)
    return dict(inputs=inputs, block_ids=block_ids, attn_gain=attn_gain, w_qkv=w_qkv, w_out=w_out, conv_gain=conv_gain, conv_in=conv_in, depthwise_w=depthwise_w, depth_gain=depth_gain, conv_out=conv_out)


EPSILON = 1e-05
query_block = 512

def layer_norm(values, weights):
    values = values.astype(jnp.float32)
    average = lax.optimization_barrier(jnp.mean(values, axis=-1, keepdims=True))
    centred = values - average
    variance = lax.optimization_barrier(jnp.mean(centred * centred, axis=-1, keepdims=True))
    return centred * lax.rsqrt(variance + EPSILON) * weights

def frame_tables(row_ids):
    earlier = lax.optimization_barrier(jnp.sum((row_ids[None, :] < row_ids[:, None]).astype(jnp.int32), axis=1))
    frame_utt = jnp.repeat(row_ids, BLOCK_LEN)
    first_frame = jnp.repeat(earlier, BLOCK_LEN) * BLOCK_LEN
    positions = jnp.arange(frame_utt.shape[0], dtype=jnp.int32) - first_frame
    return (frame_utt, positions)

def rotate(values, positions):
    half_dim = values.shape[-1] // 2
    inverse = 10000.0 ** (-jnp.arange(half_dim, dtype=jnp.float32) / half_dim)
    angles = positions.astype(jnp.float32)[:, None] * inverse[None, :]
    cosine = jnp.cos(angles)[:, None, :]
    sine_table = jnp.sin(angles)[:, None, :]
    first_half = values[..., :half_dim]
    second = values[..., half_dim:]
    return jnp.concatenate([first_half * cosine - second * sine_table, second * cosine + first_half * sine_table], axis=-1)

def project(normed, w_qkv, positions):
    projected = jnp.dot(normed, w_qkv, preferred_element_type=jnp.float32)
    shaped = projected.reshape(projected.shape[0], 3, HEAD_COUNT, HEAD_DIM)
    queries = rotate(shaped[:, 0], positions).astype(jnp.bfloat16)
    key_rows = rotate(shaped[:, 1], positions).astype(jnp.bfloat16)
    value_rows = shaped[:, 2].astype(jnp.bfloat16)
    return (queries, key_rows, value_rows)

def depthwise(gated, frame_utt, padded_utt, kernel_weights):
    length = frame_utt.shape[0]
    result = jnp.zeros((length, gated.shape[1]), jnp.float32)
    for shift_tap in range(KERNEL):
        same_utt = (padded_utt[shift_tap:shift_tap + length] == frame_utt)[:, None]
        term = kernel_weights[shift_tap][None, :] * gated[shift_tap:shift_tap + length].astype(jnp.float32)
        result = result + jnp.where(same_utt, term, 0.0)
    return result

def attend_row(queries, key_rows, value_rows, frame_utt):
    score_scale = 1.0 / math.sqrt(HEAD_DIM)
    keys_float = key_rows.astype(jnp.float32)
    values_float = value_rows.astype(jnp.float32)

    def one_block(offset):
        block_queries = lax.dynamic_slice_in_dim(queries, offset, query_block, 0).astype(jnp.float32)
        block_utt = lax.dynamic_slice_in_dim(frame_utt, offset, query_block, 0)
        scores = jnp.einsum('qhd,khd->hqk', block_queries, keys_float) * score_scale
        allowed = (block_utt[:, None] == frame_utt[None, :])[None]
        scores = jnp.where(allowed, scores, -jnp.inf)
        row_max = lax.optimization_barrier(jnp.max(scores, axis=-1, keepdims=True))
        exp_scores = jnp.exp(scores - row_max)
        row_sum = lax.optimization_barrier(jnp.sum(exp_scores, axis=-1))
        rounded = lax.optimization_barrier(exp_scores.astype(jnp.bfloat16)).astype(jnp.float32)
        weighted = jnp.einsum('hqk,khd->qhd', rounded, values_float)
        return weighted / jnp.transpose(row_sum)[:, :, None]
    block_starts = jnp.arange(0, FRAMES, query_block, dtype=jnp.int32)
    blocks = lax.map(one_block, block_starts)
    return blocks.reshape(FRAMES, HEAD_COUNT * HEAD_DIM).astype(jnp.bfloat16)

def one_row(row_inputs, row_ids, attn_gain, w_qkv, w_out, conv_gain, conv_in, depthwise_w, depth_gain, conv_out):
    frame_utt, positions = frame_tables(row_ids)
    normed = layer_norm(row_inputs, attn_gain).astype(jnp.bfloat16)
    queries, key_rows, value_rows = project(normed, w_qkv, positions)
    attended = attend_row(queries, key_rows, value_rows, frame_utt)
    residual = row_inputs.astype(jnp.float32) + jnp.dot(attended, w_out, preferred_element_type=jnp.float32)
    conv_normed = layer_norm(residual, conv_gain).astype(jnp.bfloat16)
    widened = jnp.dot(conv_normed, conv_in, preferred_element_type=jnp.float32)
    gated = (widened[:, :MODEL_DIM] * jax.nn.sigmoid(widened[:, MODEL_DIM:])).astype(jnp.bfloat16)
    half_kernel = KERNEL // 2
    padded = jnp.pad(gated, ((half_kernel, half_kernel), (0, 0)))
    padded_utt = jnp.pad(frame_utt, (half_kernel, half_kernel), constant_values=-1)
    filtered = depthwise(padded, frame_utt, padded_utt, depthwise_w)
    activated = jax.nn.silu(layer_norm(filtered, depth_gain)).astype(jnp.bfloat16)
    return (residual + jnp.dot(activated, conv_out, preferred_element_type=jnp.float32)).astype(jnp.bfloat16)

def reference(inputs, block_ids, attn_gain, w_qkv, w_out, conv_gain, conv_in, depthwise_w, depth_gain, conv_out):
    outputs = []
    for row_number in range(ROW_COUNT):
        outputs.append(one_row(inputs[row_number], block_ids[row_number], attn_gain, w_qkv, w_out, conv_gain, conv_in, depthwise_w, depth_gain, conv_out))
    return jnp.stack(outputs)
```

```python
import functools
import math

import jax
import jax.numpy as jnp
import numpy as np
from jax import lax
from jax.experimental import pallas as pl
from jax.experimental.pallas import tpu as pltpu
from jax.sharding import PartitionSpec as P

MODEL_DIM = 1536
HEAD_COUNT = 8
HEAD_DIM = 96
HALF = HEAD_DIM // 2
KERNEL = 31
BLOCK = 128
BLOCKS = 32
LONG = 24
REST = BLOCKS - LONG
HERE = 256
SHARD = 384
EPSILON = 1e-05
MESH = pl.DeviceIdType.MESH
F32 = jnp.float32
BF16 = jnp.bfloat16


def rotation_tables():
    inverse = 10000.0 ** (-np.arange(HALF, dtype=np.float64) / HALF)
    angles = np.arange(LONG * BLOCK, dtype=np.float64)[None, :] * inverse[:, None]
    pair = np.stack([np.cos(angles), np.sin(angles)])
    pair = pair.reshape(2, HALF, LONG, BLOCK).transpose(2, 0, 1, 3)
    return np.ascontiguousarray(pair).astype(np.float32)


def norm(values, gain):
    average = jnp.mean(values, axis=-1, keepdims=True)
    centred = values - average
    variance = jnp.mean(centred * centred, axis=-1, keepdims=True)
    return centred * lax.rsqrt(variance + EPSILON) * gain


def flip(index, off):
    out = index
    for bit in (1, 2, 4):
        if off & bit:
            out = out + bit - 2 * bit * ((index // bit) % 2)
    return out


def kernel(
    x_hbm, ids, attn_gain, wqkv_hbm, wout_hbm, conv_gain, cin_hbm, dw, depth_gain, cout_hbm, tab_hbm,
    out,
    xv, wq, wo, cw, co, tab, normed, send, recv, ks, vs, qs, sbuf, ostage, osend, att, resid, filt, ext, tmp,
    load_sem, wq_sem, a2a_send, a2a_recv, fwd_send, fwd_recv, o_send, o_recv,
    g_send, g_recv, s_send, s_recv, h_send, h_recv,
):
    d = lax.axis_index("dp")
    c = lax.axis_index("ctx")
    chip, core = c // 2, c % 2
    sibling = c + 1 - 2 * core
    z, yh = d // 2, d % 2
    zp, zm, z2 = (z + 1) % 4, (z + 3) % 4, (z + 2) % 4
    other = 1 - yh
    y_lo = chip % 2
    across = (2 * z + other, c + 2 - 4 * y_lo)
    up, down = (2 * zp + yh, c), (2 * zm + yh, c)
    right, left = (d, (c + 1) % 16), (d, (c + 15) % 16)
    peers = [(d, 2 * flip(chip, off) + core) for off in range(8)]

    barrier = pltpu.get_barrier_semaphore()
    cross = (d, lax.select(core == 0, (c + 15) % 16, (c + 1) % 16))
    greeted = peers[1:] + [(d, sibling), across, up, down, cross]
    for device in greeted:
        pl.semaphore_signal(barrier, inc=1, device_id=device, device_id_type=MESH)

    loads = [
        pltpu.make_async_copy(x_hbm.at[0], xv, load_sem.at[0]),
        pltpu.make_async_copy(tab_hbm, tab, load_sem.at[1]),
        pltpu.make_async_copy(wout_hbm, wo, load_sem.at[2]),
        pltpu.make_async_copy(cout_hbm, co, load_sem.at[3]),
        pltpu.make_async_copy(cin_hbm, cw.at[:, pl.ds(SHARD * d, SHARD)], load_sem.at[4]),
    ]
    loads[0].start()
    far = 1 - chip // 4
    groups = (far, chip // 4)
    wq_copies = []
    for stage in range(2):
        for kind in range(3):
            start = pl.multiple_of(768 * kind + SHARD * groups[stage], 128)
            slot = 3 * stage + kind
            copy = pltpu.make_async_copy(
                wqkv_hbm.at[:, pl.ds(start, SHARD)], wq.at[slot], wq_sem.at[slot]
            )
            copy.start()
            wq_copies.append(copy)
        if stage == 0:
            loads[1].start()
    for copy in loads[2:]:
        copy.start()

    def remote(src, dst, device, ssem, rsem):
        return pltpu.make_async_remote_copy(
            src_ref=src, dst_ref=dst, send_sem=ssem, recv_sem=rsem, device_id=device, device_id_type=MESH
        )

    half_rows = pl.ds(pl.multiple_of(768 * core, 768), 768)
    other_rows = pl.ds(pl.multiple_of(768 - 768 * core, 768), 768)

    def part(dd, rows=half_rows):
        return cw.at[rows, pl.ds(pl.multiple_of(SHARD * dd, 128), SHARD)]

    def third(dd, n):
        return part(dd, pl.ds(pl.multiple_of(768 * core + 256 * n, 256), 256))

    def gather_copy(src, dd_dst, device, n):
        return remote(src, dd_dst, device, g_send.at[n], g_recv.at[n])

    own = cin_hbm.at[half_rows]
    a_up, a_down, a_far = 2 * zp + yh, 2 * zm + yh, 2 * z2 + yh
    b_here, b_up, b_down, b_far = 2 * z + other, 2 * zp + other, 2 * zm + other, 2 * z2 + other

    pl.semaphore_wait(barrier, len(greeted))

    step_1 = [
        gather_copy(own, part(d), down, 0),
        gather_copy(own, part(d), across, 1),
        gather_copy(own, part(d), up, 2),
    ]
    for copy in step_1:
        copy.start()

    loads[0].wait()

    def norm_rows(i, _):
        rows = pl.ds(pl.multiple_of(64 * i, 64), 64)
        normed[rows, :] = norm(xv[rows, :].astype(F32), attn_gain[...]).astype(BF16)
        return _

    lax.fori_loop(0, HERE // 64, norm_rows, 0)

    place = []
    for t in range(2):
        mine = ids[0, 2 * c + t]
        earlier = jnp.int32(0)
        for j in range(BLOCKS):
            earlier = earlier + (ids[0, j] < mine).astype(jnp.int32)
        place.append(lax.min(2 * c + t - earlier, LONG - 1))
    loads[1].wait()
    cosine = jnp.concatenate([tab[place[0], 0], tab[place[1], 0]], axis=1)
    sine = jnp.concatenate([tab[place[0], 1], tab[place[1], 1]], axis=1)
    scale = math.log2(math.e) / math.sqrt(HEAD_DIM)

    sends = {}
    for stage in range(2):
        group = groups[stage]
        for kind in range(3):
            slot = 3 * stage + kind
            wq_copies[slot].wait()
            turned = jnp.transpose(jnp.dot(normed[...], wq[slot], preferred_element_type=F32))
            for i in range(4):
                first = turned[96 * i : 96 * i + 48]
                second = turned[96 * i + 48 : 96 * i + 96]
                if kind < 2:
                    first, second = first * cosine - second * sine, second * cosine + first * sine
                if kind == 0:
                    first, second = first * scale, second * scale
                first, second = first.astype(BF16), second.astype(BF16)
                for t in range(2):
                    lanes = slice(BLOCK * t, BLOCK * t + BLOCK)
                    send[4 * group + i, t, kind, 0:48, :] = first[:, lanes]
                    send[4 * group + i, t, kind, 48:96, :] = second[:, lanes]
        for off in (range(4, 8) if stage == 0 else range(1, 4)):
            sends[off] = remote(
                send.at[flip(chip, off)], recv.at[pl.ds(2 * c, 2)], peers[off],
                a2a_send.at[off], a2a_recv.at[off],
            )
            sends[off].start()
    keep = pltpu.make_async_copy(send.at[chip], recv.at[pl.ds(2 * c, 2)], load_sem.at[5])
    keep.start()
    forwards = {
        0: remote(
            send.at[chip, :, pl.ds(1, 2)], recv.at[pl.ds(2 * c, 2), pl.ds(1, 2)], (d, sibling),
            fwd_send.at[0], fwd_recv.at[0],
        )
    }
    forwards[0].start()

    sib_copies = []

    def to_sibling(ref, n):
        copy = remote(ref, ref, (d, sibling), s_send.at[n], s_recv.at[n])
        copy.start()
        sib_copies.append(copy)

    def forward(off):
        source = 2 * flip(chip, off) + core
        remote(
            send.at[0], recv.at[pl.ds(2 * source, 2)], peers[off], a2a_send.at[off], a2a_recv.at[off]
        ).wait_recv()
        block = recv.at[pl.ds(2 * source, 2), pl.ds(1, 2)]
        forwards[off] = remote(block, block, (d, sibling), fwd_send.at[off], fwd_recv.at[off])
        forwards[off].start()

    def gather_wait(ref, n):
        remote(ref, ref, up, g_send.at[n], g_recv.at[n]).wait_recv()

    for off in range(4, 8):
        forward(off)

    gather_wait(part(a_up), 0)
    gather_wait(part(b_here), 1)
    step_2 = [
        gather_copy(part(a_up), part(a_up), down, 3),
        gather_copy(part(a_up), part(a_up), across, 4),
        gather_copy(part(b_here), part(b_here), up, 5),
    ]
    for copy in step_2:
        copy.start()
    gather_wait(part(a_down), 2)
    for off in range(1, 4):
        forward(off)
    to_sibling(part(a_up), 0)
    to_sibling(part(b_here), 1)
    to_sibling(part(a_down), 2)

    keep.wait()
    for off in range(8):
        source = 2 * flip(chip, off) + 1 - core
        block = recv.at[pl.ds(2 * source, 2), pl.ds(1, 2)]
        remote(block, block, (d, sibling), fwd_send.at[off], fwd_recv.at[off]).wait_recv()

    first_long = jnp.int32(0)
    for j in range(REST):
        first_long = first_long + (ids[0, j] != ids[0, BLOCKS // 2]).astype(jnp.int32)
    first_query = jnp.int32(0)
    for u in range(REST // 2):
        first_query = first_query + (4 * (u // 2) + 2 * core + u % 2 < first_long).astype(jnp.int32)

    pad = jnp.zeros((BLOCK - HEAD_DIM, BLOCK), BF16)
    vs[96:112, :] = jnp.ones((16, BLOCKS * BLOCK), BF16)

    def place_keys(j, _):
        block = lax.rem(first_long + j, BLOCKS)
        spot = pl.ds(pl.multiple_of(BLOCK * j, BLOCK), BLOCK)
        ks[spot, :] = jnp.transpose(jnp.concatenate([recv[block, 1], pad], axis=0))
        vs[0:96, spot] = recv[block, 2]
        return _

    lax.fori_loop(0, BLOCKS, place_keys, 0)

    def place_queries(j, _):
        u = lax.rem(first_query + j, 16)
        block = 4 * (u // 2) + 2 * core + u % 2
        qs[:, pl.ds(pl.multiple_of(BLOCK * j, BLOCK), BLOCK)] = jnp.concatenate([recv[block, 0], pad], axis=0)
        return _

    lax.fori_loop(0, 16, place_queries, 0)

    def finish(total, j):
        attended = (total[0:96] / total[96:97]).astype(BF16)
        ostage[2 * j] = attended[:, :BLOCK]
        ostage[2 * j + 1] = attended[:, BLOCK:]

    def long_tile(j, _):
        queries = qs[:, pl.ds(pl.multiple_of(256 * j, 256), 256)]
        top = None
        for k in range(6):
            scores = jnp.dot(ks[512 * k : 512 * k + 512, :], queries, preferred_element_type=F32)
            sbuf[512 * k : 512 * k + 512, :] = scores
            peak = jnp.max(scores, axis=0, keepdims=True)
            top = peak if top is None else jnp.maximum(top, peak)
        total = jnp.zeros((112, 256), F32)
        for k in range(6):
            weights = jnp.exp2(sbuf[512 * k : 512 * k + 512, :] - top).astype(BF16)
            total += jnp.dot(vs[:, 512 * k : 512 * k + 512], weights, preferred_element_type=F32)
        finish(total, j)
        return _

    lax.fori_loop(0, 6, long_tile, 0)

    lane = lax.broadcasted_iota(jnp.int32, (1, 256), 1)
    for j in range(6, 8):
        queries = qs[:, 256 * j : 256 * j + 256]
        marks = []
        for t in range(2):
            u = lax.rem(first_query + 2 * j + t, 16)
            marks.append(ids[0, 4 * (u // 2) + 2 * core + u % 2])
        query_ids = jnp.where(lane < BLOCK, marks[0], marks[1])
        top = None
        for k in range(REST):
            key_id = ids[0, lax.rem(first_long + LONG + k, BLOCKS)]
            rows = pl.ds(BLOCK * (LONG + k), BLOCK)
            scores = jnp.dot(ks[rows, :], queries, preferred_element_type=F32)
            scores = jnp.where(query_ids == key_id, scores, -jnp.inf)
            sbuf[BLOCK * k : BLOCK * k + BLOCK, :] = scores
            peak = jnp.max(scores, axis=0, keepdims=True)
            top = peak if top is None else jnp.maximum(top, peak)
        weights = jnp.exp2(sbuf[0 : REST * BLOCK, :] - top).astype(BF16)
        finish(jnp.dot(vs[:, LONG * BLOCK :], weights, preferred_element_type=F32), j)

    def unplace(u, _):
        osend[u] = ostage[lax.rem(u - first_query + 16, 16)]
        return _

    lax.fori_loop(0, 16, unplace, 0)
    o_copies = {}
    for off in (6, 7, 4, 5, 2, 3, 1):
        to = flip(chip, off)
        o_copies[off] = remote(
            osend.at[pl.ds(2 * to, 2)], att.at[chip], peers[off], o_send.at[off], o_recv.at[off]
        )
        o_copies[off].start()
    o_keep = pltpu.make_async_copy(osend.at[pl.ds(2 * chip, 2)], att.at[chip], load_sem.at[6])
    o_keep.start()

    gather_wait(part(a_far), 3)
    gather_wait(part(b_up), 4)
    gather_wait(part(b_down), 5)
    step_3 = [
        gather_copy(third(a_far, 0), third(a_far, 0), across, 6),
        gather_copy(third(b_up, 1), third(b_up, 1), down, 7),
        gather_copy(third(b_down, 2), third(b_down, 2), up, 8),
    ]
    for copy in step_3:
        copy.start()
    to_sibling(part(a_far), 3)
    to_sibling(part(b_up), 4)
    to_sibling(part(b_down), 5)

    loads[2].wait()
    o_keep.wait()
    for off in range(1, 8):
        source = flip(chip, off)
        remote(att.at[source], att.at[source], peers[off], o_send.at[off], o_recv.at[off]).wait_recv()

    for t in range(2):
        turned = jnp.concatenate([att[h, t] for h in range(8)], axis=0)
        rows = slice(BLOCK * t, BLOCK * t + BLOCK)
        normed[rows, 0:768] = jnp.transpose(turned)

    def add_out(i, _):
        cols = pl.ds(pl.multiple_of(512 * i, 512), 512)
        resid[:, cols] = xv[:, cols].astype(F32) + jnp.dot(
            normed[:, 0:768], wo[:, cols], preferred_element_type=F32
        )
        return _

    lax.fori_loop(0, 3, add_out, 0)

    def norm_residual(i, _):
        rows = pl.ds(pl.multiple_of(64 * i, 64), 64)
        normed[rows, :] = norm(resid[rows, :], conv_gain[...]).astype(BF16)
        return _

    lax.fori_loop(0, HERE // 64, norm_residual, 0)

    for n in range(3):
        gather_wait(third(b_far, n), 6 + n)
    to_sibling(part(b_far), 6)
    loads[4].wait()
    for n, dd in enumerate((a_up, b_here, a_down, a_far, b_up, b_down, b_far)):
        ref = part(dd, other_rows)
        remote(ref, ref, (d, sibling), s_send.at[n], s_recv.at[n]).wait_recv()

    def edge_copies(i):
        cols = pl.ds(pl.multiple_of(256 * i, 256), 256)
        return [
            remote(ext.at[pl.ds(256, 16), cols], ext.at[pl.ds(0, 16), cols], right, h_send.at[0, i], h_recv.at[0, i]),
            remote(ext.at[pl.ds(16, 16), cols], ext.at[pl.ds(272, 16), cols], left, h_send.at[1, i], h_recv.at[1, i]),
        ]

    def gate(i, _):
        cols = pl.ds(pl.multiple_of(256 * i, 256), 256)
        gate_cols = pl.ds(pl.multiple_of(MODEL_DIM + 256 * i, 256), 256)
        value = jnp.dot(normed[...], cw[:, cols], preferred_element_type=F32)
        gates = jnp.dot(normed[...], cw[:, gate_cols], preferred_element_type=F32)
        ext[16:272, cols] = (value * jax.nn.sigmoid(gates)).astype(BF16)
        for copy in edge_copies(i):
            copy.start()
        return _

    lax.fori_loop(0, 6, gate, 0)

    here_0, here_1 = ids[0, 2 * c], ids[0, 2 * c + 1]
    before = ids[0, lax.max(2 * c - 1, 0)]
    after = ids[0, lax.min(2 * c + 2, BLOCKS - 1)]
    inner = here_0 == here_1
    keeps = (
        (jnp.logical_and(c > 0, before == here_0), inner),
        (inner, jnp.logical_and(c < 15, after == here_1)),
    )

    def filter_lanes(i, _):
        cols = pl.ds(pl.multiple_of(BLOCK * i, BLOCK), BLOCK)
        for t in range(2):
            head = ext[BLOCK * t : BLOCK * t + 16, cols].astype(F32)
            tail = ext[BLOCK * t + 144 : BLOCK * t + 160, cols].astype(F32)
            tmp[t, 0:16, :] = jnp.where(keeps[t][0], head, 0.0)
            tmp[t, 16:144, :] = ext[BLOCK * t + 16 : BLOCK * t + 144, cols].astype(F32)
            tmp[t, 144:160, :] = jnp.where(keeps[t][1], tail, 0.0)
            total = jnp.zeros((BLOCK, BLOCK), F32)
            for tap in range(KERNEL):
                total += dw[tap : tap + 1, cols] * tmp[t, tap + 1 : tap + 1 + BLOCK, :]
            filt[BLOCK * t : BLOCK * t + BLOCK, cols] = total
        return _

    def filter_pair(i, _):
        for copy in edge_copies(i):
            copy.wait_recv()
        lax.fori_loop(2 * i, 2 * i + 2, filter_lanes, 0)
        return _

    lax.fori_loop(0, 6, filter_pair, 0)

    def norm_filtered(i, _):
        rows = pl.ds(pl.multiple_of(64 * i, 64), 64)
        values = norm(filt[rows, :], depth_gain[...])
        normed[rows, :] = (values / (1.0 + jnp.exp(-values))).astype(BF16)
        return _

    lax.fori_loop(0, HERE // 64, norm_filtered, 0)

    loads[3].wait()

    def add_conv(i, _):
        cols = pl.ds(pl.multiple_of(512 * i, 512), 512)
        out[0, :, cols] = (
            resid[:, cols] + jnp.dot(normed[...], co[:, cols], preferred_element_type=F32)
        ).astype(BF16)
        return _

    lax.fori_loop(0, 3, add_conv, 0)

    for copy in step_1 + step_2 + step_3 + sib_copies:
        copy.wait_send()
    for copies in (sends, forwards, o_copies):
        for copy in copies.values():
            copy.wait_send()

    def drain(i, _):
        for copy in edge_copies(i):
            copy.wait_send()
        return _

    lax.fori_loop(0, 6, drain, 0)


def local(inputs, block_ids, attn_gain, w_qkv, w_out, conv_gain, conv_in, depthwise_w, depth_gain, conv_out):
    in_hbm = pl.BlockSpec(memory_space=pl.ANY)
    in_vmem = pl.BlockSpec(memory_space=pltpu.VMEM)
    in_smem = pl.BlockSpec(memory_space=pltpu.SMEM)
    dma = pltpu.SemaphoreType.DMA
    return pl.pallas_call(
        kernel,
        out_shape=jax.ShapeDtypeStruct((1, HERE, MODEL_DIM), BF16),
        in_specs=[
            in_hbm, in_smem, in_vmem, in_hbm, in_hbm, in_vmem, in_hbm, in_vmem, in_vmem, in_hbm, in_hbm,
        ],
        out_specs=in_vmem,
        scratch_shapes=[
            pltpu.VMEM((HERE, MODEL_DIM), BF16),
            pltpu.VMEM((6, MODEL_DIM, SHARD), BF16),
            pltpu.VMEM((768, MODEL_DIM), BF16),
            pltpu.VMEM((MODEL_DIM, 2 * MODEL_DIM), BF16),
            pltpu.VMEM((MODEL_DIM, MODEL_DIM), BF16),
            pltpu.VMEM((LONG, 2, HALF, BLOCK), F32),
            pltpu.VMEM((HERE, MODEL_DIM), BF16),
            pltpu.VMEM((8, 2, 3, HEAD_DIM, BLOCK), BF16),
            pltpu.VMEM((BLOCKS, 3, HEAD_DIM, BLOCK), BF16),
            pltpu.VMEM((BLOCKS * BLOCK, BLOCK), BF16),
            pltpu.VMEM((112, BLOCKS * BLOCK), BF16),
            pltpu.VMEM((BLOCK, 16 * BLOCK), BF16),
            pltpu.VMEM((LONG * BLOCK, 256), F32),
            pltpu.VMEM((16, HEAD_DIM, BLOCK), BF16),
            pltpu.VMEM((16, HEAD_DIM, BLOCK), BF16),
            pltpu.VMEM((8, 2, HEAD_DIM, BLOCK), BF16),
            pltpu.VMEM((HERE, MODEL_DIM), F32),
            pltpu.VMEM((HERE, MODEL_DIM), F32),
            pltpu.VMEM((HERE + 32, MODEL_DIM), BF16),
            pltpu.VMEM((2, 160, BLOCK), F32),
            dma((7,)), dma((6,)), dma((8,)), dma((8,)), dma((8,)), dma((8,)), dma((8,)), dma((8,)),
            dma((9,)), dma((9,)), dma((7,)), dma((7,)), dma((2, 6)), dma((2, 6)),
        ],
        compiler_params=pltpu.CompilerParams(
            collective_id=0, has_side_effects=True, vmem_limit_bytes=56 * 1024 * 1024
        ),
        name="conformer",
    )(
        inputs, block_ids, attn_gain[None], w_qkv, w_out, conv_gain[None], conv_in, depthwise_w,
        depth_gain[None], conv_out, jnp.asarray(rotation_tables()),
    )


def solution(mesh):
    return jax.shard_map(
        local,
        mesh=mesh,
        in_specs=(
            P("dp", "ctx", None),
            P("dp", None),
            P(),
            P(),
            P(),
            P(),
            P(None, "dp"),
            P(),
            P(),
            P(),
        ),
        out_specs=P("dp", "ctx", None),
        check_vma=False,
    )
```

```python
import functools
import math

import jax
import jax.numpy as jnp
import numpy as np
from jax import lax
from jax.experimental import pallas as pl
from jax.experimental.pallas import tpu as pltpu
from jax.sharding import PartitionSpec as P

MODEL_DIM = 1536
HEAD_COUNT = 8
HEAD_DIM = 96
HALF = HEAD_DIM // 2
KERNEL = 31
BLOCK = 128
BLOCKS = 32
LONG = 24
AWAY = -1e30
HERE = 256
SHARD = 384
EPSILON = 1e-05
MESH = pl.DeviceIdType.MESH
F32 = jnp.float32
BF16 = jnp.bfloat16


def rotation_tables():
    inverse = 10000.0 ** (-np.arange(HALF, dtype=np.float64) / HALF)
    angles = np.arange(LONG * BLOCK, dtype=np.float64)[None, :] * inverse[:, None]
    pair = np.stack([np.cos(angles), np.sin(angles)])
    pair = pair.reshape(2, HALF, LONG, BLOCK).transpose(2, 0, 1, 3)
    return np.ascontiguousarray(pair).astype(np.float32)


def norm(values, gain):
    average = jnp.mean(values, axis=-1, keepdims=True)
    centred = values - average
    variance = jnp.mean(centred * centred, axis=-1, keepdims=True)
    return centred * lax.rsqrt(variance + EPSILON) * gain


def flip(index, off):
    out = index
    for bit in (1, 2, 4):
        out = out + bit * ((off // bit) % 2) * (1 - 2 * ((index // bit) % 2))
    return out


def kernel(
    x_hbm, ids, attn_gain, wqkv_hbm, wout_hbm, conv_gain, cin_hbm, dw, depth_gain, cout_hbm, tab_hbm,
    out,
    xv, wq, wo, cw, co, tab, normed, sq, skv, qbuf, kvbuf, kn, peaks, totals, osend, att, resid, filt, ext, tmp,
    load_sem, wq_sem, q_send, q_recv, kv_send, kv_recv, fwd_send, fwd_recv, o_send, o_recv,
    g_send, g_recv, s_send, s_recv, h_send, h_recv,
):
    d = lax.axis_index("dp")
    c = lax.axis_index("ctx")
    chip, core = c // 2, c % 2
    sibling = (d, c + 1 - 2 * core)
    z, yh = d // 2, d % 2
    zp, zm, z2 = (z + 1) % 4, (z + 3) % 4, (z + 2) % 4
    other = 1 - yh
    across = (2 * z + other, c + 2 - 4 * (chip % 2))
    up, down = (2 * zp + yh, c), (2 * zm + yh, c)
    right, left = (d, (c + 1) % 16), (d, (c + 15) % 16)

    def peer(off):
        return (d, 2 * flip(chip, off) + core)

    barrier = pltpu.get_barrier_semaphore()
    cross = (d, lax.select(core == 0, (c + 15) % 16, (c + 1) % 16))
    greeted = [peer(off) for off in range(1, 8)] + [sibling, across, up, down, cross]
    for device in greeted:
        pl.semaphore_signal(barrier, inc=1, device_id=device, device_id_type=MESH)

    loads = [
        pltpu.make_async_copy(x_hbm.at[0], xv, load_sem.at[0]),
        pltpu.make_async_copy(tab_hbm, tab, load_sem.at[1]),
        pltpu.make_async_copy(wout_hbm, wo, load_sem.at[2]),
        pltpu.make_async_copy(cout_hbm, co, load_sem.at[3]),
        pltpu.make_async_copy(cin_hbm, cw.at[:, pl.ds(SHARD * d, SHARD)], load_sem.at[4]),
    ]
    loads[0].start()
    far, near = 1 - chip // 4, chip // 4
    steps = ((0, far), (0, near), (1, far), (2, far), (1, near), (2, near))
    wq_copies = []
    for slot, (kind, group) in enumerate(steps):
        start = pl.multiple_of(768 * kind + SHARD * group, 128)
        copy = pltpu.make_async_copy(wqkv_hbm.at[:, pl.ds(start, SHARD)], wq.at[slot], wq_sem.at[slot])
        copy.start()
        wq_copies.append(copy)
        if slot == 0:
            loads[1].start()
    for copy in loads[2:]:
        copy.start()

    def remote(src, dst, device, ssem, rsem):
        return pltpu.make_async_remote_copy(
            src_ref=src, dst_ref=dst, send_sem=ssem, recv_sem=rsem, device_id=device, device_id_type=MESH
        )

    loads[0].wait()

    def norm_rows(i, _):
        rows = pl.ds(pl.multiple_of(64 * i, 64), 64)
        normed[rows, :] = norm(xv[rows, :].astype(F32), attn_gain[...]).astype(BF16)
        return _

    lax.fori_loop(0, HERE // 64, norm_rows, 0)

    a_up, a_down, a_far = 2 * zp + yh, 2 * zm + yh, 2 * z2 + yh
    b_here, b_up, b_down, b_far = 2 * z + other, 2 * zp + other, 2 * zm + other, 2 * z2 + other

    def piece(dd, p, of=core):
        return cw.at[pl.ds(pl.multiple_of(768 * of + 384 * p, 384), 384), pl.ds(pl.multiple_of(SHARD * dd, 128), SHARD)]

    def third(dd, p, n):
        rows = pl.ds(pl.multiple_of(768 * core + 384 * p + 128 * n, 128), 128)
        return cw.at[rows, pl.ds(pl.multiple_of(SHARD * dd, 128), SHARD)]

    def gather(src, dst, device, p, n):
        return remote(src, dst, device, g_send.at[p, n], g_recv.at[p, n])

    def start_all(copies):
        for copy in copies:
            copy.start()

    def gather_wait(ref, p, n):
        remote(ref, ref, up, g_send.at[p, n], g_recv.at[p, n]).wait_recv()

    def to_sibling(dd, p, n):
        return remote(piece(dd, p), piece(dd, p), sibling, s_send.at[p, n], s_recv.at[p, n])

    def from_sibling(dd, n):
        for p in range(2):
            ref = piece(dd, p, 1 - core)
            remote(ref, ref, sibling, s_send.at[p, n], s_recv.at[p, n]).wait_recv()

    def gather_1(p):
        own = cin_hbm.at[pl.ds(pl.multiple_of(768 * core + 384 * p, 384), 384)]
        return [
            gather(own, piece(d, p), down, p, 0),
            gather(own, piece(d, p), across, p, 1),
            gather(own, piece(d, p), up, p, 2),
        ]

    def gather_2(p):
        return [
            gather(piece(a_up, p), piece(a_up, p), down, p, 3),
            gather(piece(a_up, p), piece(a_up, p), across, p, 4),
            gather(piece(b_here, p), piece(b_here, p), up, p, 5),
            to_sibling(a_up, p, 0),
            to_sibling(b_here, p, 1),
            to_sibling(a_down, p, 2),
        ]

    def gather_3(p):
        return [
            gather(third(a_far, p, 0), third(a_far, p, 0), across, p, 6),
            gather(third(b_up, p, 1), third(b_up, p, 1), down, p, 7),
            gather(third(b_down, p, 2), third(b_down, p, 2), up, p, 8),
            to_sibling(a_far, p, 3),
            to_sibling(b_up, p, 4),
            to_sibling(b_down, p, 5),
        ]

    def gather_4(p):
        return [to_sibling(b_far, p, 6)]

    def run_2(p):
        gather_wait(piece(a_up, p), p, 0)
        gather_wait(piece(b_here, p), p, 1)
        gather_wait(piece(a_down, p), p, 2)
        start_all(gather_2(p))

    def run_3(p):
        gather_wait(piece(a_far, p), p, 3)
        gather_wait(piece(b_up, p), p, 4)
        gather_wait(piece(b_down, p), p, 5)
        start_all(gather_3(p))

    def run_4(p):
        for n in range(3):
            gather_wait(third(b_far, p, n), p, 6 + n)
        start_all(gather_4(p))

    place = []
    for t in range(2):
        mine = ids[0, 2 * c + t]
        earlier = jnp.int32(0)
        for j in range(BLOCKS):
            earlier = earlier + (ids[0, j] < mine).astype(jnp.int32)
        place.append(lax.min(2 * c + t - earlier, LONG - 1))
    loads[1].wait()
    cosine = jnp.concatenate([tab[place[0], 0], tab[place[1], 0]], axis=1)
    sine = jnp.concatenate([tab[place[0], 1], tab[place[1], 1]], axis=1)
    scale = math.log2(math.e) / math.sqrt(HEAD_DIM)

    def q_slot(i):
        return qbuf.at[i, pl.ds(0, HEAD_DIM)]

    def kv_slot(i, of):
        return kvbuf.at[i, :, pl.ds(0, HEAD_DIM), pl.ds(pl.multiple_of(HERE * of, HERE), HERE)]

    sends = []
    for slot, (kind, group) in enumerate(steps):
        wq_copies[slot].wait()
        turned = jnp.transpose(jnp.dot(normed[...], wq[slot], preferred_element_type=F32))
        for i in range(4):
            first = turned[96 * i : 96 * i + 48]
            second = turned[96 * i + 48 : 96 * i + 96]
            if kind < 2:
                first, second = first * cosine - second * sine, second * cosine + first * sine
            if kind == 0:
                sq[4 * group + i, 0:48, :] = (first * scale).astype(BF16)
                sq[4 * group + i, 48:96, :] = (second * scale).astype(BF16)
            else:
                skv[4 * group + i, kind - 1, 0:48, :] = first.astype(BF16)
                skv[4 * group + i, kind - 1, 48:96, :] = second.astype(BF16)
        if slot == 3:
            pl.semaphore_wait(barrier, len(greeted))
            for off in range(1, 8):
                to = flip(chip, off)
                sends.append(remote(sq.at[to], q_slot(chip), peer(off), q_send.at[off], q_recv.at[off]))
                sends[-1].start()
            start_all(gather_1(0))
            start_all(gather_1(1))
        if slot in (3, 5):
            for off in (range(4, 8) if slot == 3 else range(1, 4)):
                to = flip(chip, off)
                sends.append(remote(skv.at[to], kv_slot(chip, core), peer(off), kv_send.at[off], kv_recv.at[off]))
                sends[-1].start()
    keep_q = pltpu.make_async_copy(sq.at[chip], q_slot(chip), load_sem.at[5])
    keep_kv = pltpu.make_async_copy(skv.at[chip], kv_slot(chip, core), load_sem.at[6])
    keep_q.start()
    keep_kv.start()

    def forward(off, src):
        return remote(src, kv_slot(flip(chip, off), core), sibling, fwd_send.at[off], fwd_recv.at[off])

    forward(0, skv.at[chip]).start()

    row = lax.broadcasted_iota(jnp.int32, (BLOCK - HEAD_DIM, BLOCK), 0)

    def mark_keys(j, _):
        spot = pl.ds(pl.multiple_of(BLOCK * (j % 4), BLOCK), BLOCK)
        kvbuf[j // 4, 0, HEAD_DIM:, spot] = jnp.where(row == ids[0, j], 1.0, 0.0).astype(BF16)
        kvbuf[j // 4, 1, HEAD_DIM:, spot] = jnp.ones((BLOCK - HEAD_DIM, BLOCK), BF16)
        return _

    def mark_queries(j, _):
        spot = pl.ds(pl.multiple_of(BLOCK * (j % 2), BLOCK), BLOCK)
        mine = ids[0, 4 * (j // 2) + 2 * core + j % 2]
        qbuf[j // 2, HEAD_DIM:, spot] = jnp.where(row == mine, 0.0, AWAY).astype(BF16)
        return _

    lax.fori_loop(0, BLOCKS, mark_keys, 0)
    lax.fori_loop(0, 16, mark_queries, 0)
    peaks[...] = jnp.full(peaks.shape, -3e38, F32)
    totals[...] = jnp.zeros(totals.shape, F32)

    keep_q.wait()
    for off in range(1, 8):
        slot = q_slot(flip(chip, off))
        remote(slot, slot, peer(off), q_send.at[off], q_recv.at[off]).wait_recv()
    keep_kv.wait()

    def order(n):
        return lax.select(n < 5, n + 3, n - 4)

    def arrive(off):
        slot = kv_slot(flip(chip, off), core)
        remote(slot, slot, peer(off), kv_send.at[off], kv_recv.at[off]).wait_recv()
        forward(off, slot).start()

    def keys_of(off):
        source = flip(chip, off)
        slot = kv_slot(source, 1 - core)
        remote(slot, slot, sibling, fwd_send.at[off], fwd_recv.at[off]).wait_recv()
        kn[...] = jnp.transpose(kvbuf[source, 0])
        return source

    def attend(source, tiles, last=False):
        scores = [jnp.dot(kn[...], qbuf[i], preferred_element_type=F32) for i in tiles]
        results = []
        for i, score in zip(tiles, scores):
            old = peaks[i]
            top = jnp.maximum(old, jnp.max(score, axis=0, keepdims=True))
            if not last:
                peaks[i] = top
            weights = jnp.exp2(score - top).astype(BF16)
            fresh = jnp.dot(kvbuf[source, 1, 0:112, :], weights, preferred_element_type=F32)
            results.append(totals[i] * jnp.exp2(old - top) + fresh)
        return results

    def use_source(n, _):
        arrive(order(n + 1))
        pl.when(n == 2)(lambda: run_2(0))
        pl.when(n == 5)(lambda: run_2(1))
        source = keys_of(lax.select(n == 0, 0, order(n)))
        for i, total in enumerate(attend(source, range(8))):
            totals[i] = total
        return _

    lax.fori_loop(0, 7, use_source, 0)
    source = keys_of(order(7))

    def o_copy(i, off):
        return remote(osend.at[i], att.at[chip], (d, 2 * i + core), o_send.at[off], o_recv.at[off])

    for offs in ((6, 7, 4, 5), (2, 3, 1, 0)):
        tiles = [flip(chip, off) for off in offs]
        for off, i, total in zip(offs, tiles, attend(source, tiles, last=True)):
            osend[i] = (total[0:96] / total[96:97]).astype(BF16)
            if off:
                o_copy(i, off).start()
    o_keep = pltpu.make_async_copy(osend.at[chip], att.at[chip], load_sem.at[7])
    o_keep.start()

    run_3(0)
    loads[2].wait()
    o_keep.wait()
    for off in range(1, 8):
        slot = att.at[flip(chip, off)]
        remote(slot, slot, peer(off), o_send.at[off], o_recv.at[off]).wait_recv()
    normed[:, 0:768] = jnp.transpose(att[...].reshape(768, HERE))

    def add_out(i, _):
        cols = pl.ds(pl.multiple_of(512 * i, 512), 512)
        resid[:, cols] = xv[:, cols].astype(F32) + jnp.dot(
            normed[:, 0:768], wo[:, cols], preferred_element_type=F32
        )
        return _

    lax.fori_loop(0, 3, add_out, 0)
    run_3(1)

    def norm_residual(i, _):
        rows = pl.ds(pl.multiple_of(64 * i, 64), 64)
        normed[rows, :] = norm(resid[rows, :], conv_gain[...]).astype(BF16)
        return _

    lax.fori_loop(0, HERE // 64, norm_residual, 0)

    def edge_copies(n, v):
        cols = pl.ds(pl.multiple_of(SHARD * v, 128), SHARD)
        return [
            remote(ext.at[pl.ds(256, 16), cols], ext.at[pl.ds(0, 16), cols], right, h_send.at[0, n], h_recv.at[0, n]),
            remote(ext.at[pl.ds(16, 16), cols], ext.at[pl.ds(272, 16), cols], left, h_send.at[1, n], h_recv.at[1, n]),
        ]

    edges = []

    def gate(n, v):
        cols = pl.ds(pl.multiple_of(SHARD * v, 128), SHARD)
        gate_cols = pl.ds(pl.multiple_of(MODEL_DIM + SHARD * v, 128), SHARD)
        value = jnp.dot(normed[...], cw[:, cols], preferred_element_type=F32)
        gates = jnp.dot(normed[...], cw[:, gate_cols], preferred_element_type=F32)
        ext[16:272, cols] = (value * jax.nn.sigmoid(gates)).astype(BF16)
        for copy in edge_copies(n, v):
            copy.start()
            edges.append(copy)

    here_0, here_1 = ids[0, 2 * c], ids[0, 2 * c + 1]
    before = ids[0, lax.max(2 * c - 1, 0)]
    after = ids[0, lax.min(2 * c + 2, BLOCKS - 1)]
    inner = here_0 == here_1
    keeps = (
        (jnp.logical_and(c > 0, before == here_0), inner),
        (inner, jnp.logical_and(c < 15, after == here_1)),
    )

    def taps(n, v):
        for copy in edge_copies(n, v):
            copy.wait_recv()

        def filter_lanes(i, _):
            cols = pl.ds(pl.multiple_of(SHARD * v + BLOCK * i, BLOCK), BLOCK)
            for t in range(2):
                head = ext[BLOCK * t : BLOCK * t + 16, cols].astype(F32)
                tail = ext[BLOCK * t + 144 : BLOCK * t + 160, cols].astype(F32)
                tmp[t, 0:16, :] = jnp.where(keeps[t][0], head, 0.0)
                tmp[t, 16:144, :] = ext[BLOCK * t + 16 : BLOCK * t + 144, cols].astype(F32)
                tmp[t, 144:160, :] = jnp.where(keeps[t][1], tail, 0.0)
                total = jnp.zeros((BLOCK, BLOCK), F32)
                for tap in range(KERNEL):
                    total += dw[tap : tap + 1, cols] * tmp[t, tap + 1 : tap + 1 + BLOCK, :]
                filt[BLOCK * t : BLOCK * t + BLOCK, cols] = total
            return _

        lax.fori_loop(0, 3, filter_lanes, 0)

    groups = (a_up % 4, b_up % 4, d % 4, b_here % 4)
    for n in (0, 2):
        from_sibling((a_up, 0, a_down)[n], n)
    gate(0, groups[0])
    for n, dd in ((4, b_up), (5, b_down)):
        from_sibling(dd, n)
    gate(1, groups[1])
    run_4(0)
    loads[4].wait()
    from_sibling(a_far, 3)
    gate(2, groups[2])
    run_4(1)
    taps(0, groups[0])
    for n, dd in ((1, b_here), (6, b_far)):
        from_sibling(dd, n)
    gate(3, groups[3])
    for n in range(1, 4):
        taps(n, groups[n])

    def norm_filtered(i, _):
        rows = pl.ds(pl.multiple_of(64 * i, 64), 64)
        values = norm(filt[rows, :], depth_gain[...])
        normed[rows, :] = (values / (1.0 + jnp.exp(-values))).astype(BF16)
        return _

    lax.fori_loop(0, HERE // 64, norm_filtered, 0)

    loads[3].wait()

    def add_conv(i, _):
        cols = pl.ds(pl.multiple_of(512 * i, 512), 512)
        out[0, :, cols] = (
            resid[:, cols] + jnp.dot(normed[...], co[:, cols], preferred_element_type=F32)
        ).astype(BF16)
        return _

    lax.fori_loop(0, 3, add_conv, 0)

    gathers = [copy for p in range(2) for step in (gather_1, gather_2, gather_3, gather_4) for copy in step(p)]
    for copy in gathers + sends + edges:
        copy.wait_send()
    forward(0, skv.at[chip]).wait_send()

    def drain(off, _):
        forward(off, kv_slot(flip(chip, off), core)).wait_send()
        o_copy(flip(chip, off), off).wait_send()
        return _

    lax.fori_loop(1, 8, drain, 0)


def local(inputs, block_ids, attn_gain, w_qkv, w_out, conv_gain, conv_in, depthwise_w, depth_gain, conv_out):
    in_hbm = pl.BlockSpec(memory_space=pl.ANY)
    in_vmem = pl.BlockSpec(memory_space=pltpu.VMEM)
    in_smem = pl.BlockSpec(memory_space=pltpu.SMEM)
    dma = pltpu.SemaphoreType.DMA
    return pl.pallas_call(
        kernel,
        out_shape=jax.ShapeDtypeStruct((1, HERE, MODEL_DIM), BF16),
        in_specs=[
            in_hbm, in_smem, in_vmem, in_hbm, in_hbm, in_vmem, in_hbm, in_vmem, in_vmem, in_hbm, in_hbm,
        ],
        out_specs=in_vmem,
        scratch_shapes=[
            pltpu.VMEM((HERE, MODEL_DIM), BF16),
            pltpu.VMEM((6, MODEL_DIM, SHARD), BF16),
            pltpu.VMEM((768, MODEL_DIM), BF16),
            pltpu.VMEM((MODEL_DIM, 2 * MODEL_DIM), BF16),
            pltpu.VMEM((MODEL_DIM, MODEL_DIM), BF16),
            pltpu.VMEM((LONG, 2, HALF, BLOCK), F32),
            pltpu.VMEM((HERE, MODEL_DIM), BF16),
            pltpu.VMEM((8, HEAD_DIM, HERE), BF16),
            pltpu.VMEM((8, 2, HEAD_DIM, HERE), BF16),
            pltpu.VMEM((8, BLOCK, HERE), BF16),
            pltpu.VMEM((8, 2, BLOCK, 2 * HERE), BF16),
            pltpu.VMEM((2 * HERE, BLOCK), BF16),
            pltpu.VMEM((8, 1, HERE), F32),
            pltpu.VMEM((8, 112, HERE), F32),
            pltpu.VMEM((8, HEAD_DIM, HERE), BF16),
            pltpu.VMEM((8, HEAD_DIM, HERE), BF16),
            pltpu.VMEM((HERE, MODEL_DIM), F32),
            pltpu.VMEM((HERE, MODEL_DIM), F32),
            pltpu.VMEM((HERE + 32, MODEL_DIM), BF16),
            pltpu.VMEM((2, 160, BLOCK), F32),
            dma((8,)), dma((6,)), dma((8,)), dma((8,)), dma((8,)), dma((8,)), dma((8,)), dma((8,)), dma((8,)), dma((8,)),
            dma((2, 9)), dma((2, 9)), dma((2, 7)), dma((2, 7)), dma((2, 4)), dma((2, 4)),
        ],
        compiler_params=pltpu.CompilerParams(
            collective_id=0, has_side_effects=True, vmem_limit_bytes=56 * 1024 * 1024
        ),
        name="conformer",
    )(
        inputs, block_ids, attn_gain, w_qkv, w_out, conv_gain, conv_in, depthwise_w,
        depth_gain, conv_out, jnp.asarray(rotation_tables()),
    )


def solution(mesh):
    return jax.shard_map(
        local,
        mesh=mesh,
        in_specs=(
            P("dp", "ctx", None),
            P("dp", None),
            P(),
            P(),
            P(),
            P(),
            P(None, "dp"),
            P(),
            P(),
            P(),
        ),
        out_specs=P("dp", "ctx", None),
        check_vma=False,
    )
```

```python
import functools
import math

import jax
import jax.numpy as jnp
import numpy as np
from jax import lax
from jax.experimental import pallas as pl
from jax.experimental.pallas import tpu as pltpu
from jax.sharding import PartitionSpec as P

MODEL_DIM = 1536
HEAD_COUNT = 8
HEAD_DIM = 96
HALF = HEAD_DIM // 2
KERNEL = 31
BLOCK = 128
BLOCKS = 32
LONG = 24
AWAY = -1e30
HERE = 256
SHARD = 384
EPSILON = 1e-05
MESH = pl.DeviceIdType.MESH
F32 = jnp.float32
BF16 = jnp.bfloat16


def rotation_tables():
    inverse = 10000.0 ** (-np.arange(HALF, dtype=np.float64) / HALF)
    angles = np.arange(LONG * BLOCK, dtype=np.float64)[None, :] * inverse[:, None]
    pair = np.stack([np.cos(angles), np.sin(angles)])
    pair = pair.reshape(2, HALF, LONG, BLOCK).transpose(2, 0, 1, 3)
    return np.ascontiguousarray(pair).astype(np.float32)


def norm(values, gain):
    average = jnp.mean(values, axis=-1, keepdims=True)
    centred = values - average
    variance = jnp.mean(centred * centred, axis=-1, keepdims=True)
    return centred * lax.rsqrt(variance + EPSILON) * gain


def flip(index, off):
    out = index
    for bit in (1, 2, 4):
        out = out + bit * ((off // bit) % 2) * (1 - 2 * ((index // bit) % 2))
    return out


def kernel(
    x_hbm, ids_hbm, attn_hbm, wqkv_hbm, wout_hbm, conv_hbm, cin_hbm, dw_hbm, depth_hbm, cout_hbm, tab_hbm,
    out_hbm,
    ids, attn_gain, conv_gain, depth_gain, dw, out, xv, wq, wo, cw, co, tab, normed, sq, skv, qbuf, kvbuf, kn, peaks, totals, osend, att, resid, filt, ext, tmp,
    load_sem, wq_sem, q_send, q_recv, kv_send, kv_recv, fwd_send, fwd_recv, o_send, o_recv,
    g_send, g_recv, s_send, s_recv, h_send, h_recv,
):
    d = lax.axis_index("dp")
    c = lax.axis_index("ctx")
    chip, core = c // 2, c % 2
    sibling = (d, c + 1 - 2 * core)
    z, yh = d // 2, d % 2
    zp, zm, z2 = (z + 1) % 4, (z + 3) % 4, (z + 2) % 4
    other = 1 - yh
    across = (2 * z + other, c + 2 - 4 * (chip % 2))
    up, down = (2 * zp + yh, c), (2 * zm + yh, c)
    right, left = (d, (c + 1) % 16), (d, (c + 15) % 16)

    def peer(off):
        return (d, 2 * flip(chip, off) + core)

    barrier = pltpu.get_barrier_semaphore()
    cross = (d, lax.select(core == 0, (c + 15) % 16, (c + 1) % 16))
    greeted = [peer(off) for off in range(1, 8)] + [sibling, across, up, down, cross]
    for device in greeted:
        pl.semaphore_signal(barrier, inc=1, device_id=device, device_id_type=MESH)

    def shard_cols(dd):
        return pl.ds(pl.multiple_of(SHARD * (2 * (dd % 4) + dd // 4), 128), SHARD)

    loads = [
        pltpu.make_async_copy(x_hbm.at[0], xv, load_sem.at[0]),
        pltpu.make_async_copy(tab_hbm, tab, load_sem.at[1]),
        pltpu.make_async_copy(wout_hbm, wo, load_sem.at[2]),
        pltpu.make_async_copy(cout_hbm, co, load_sem.at[3]),
        pltpu.make_async_copy(cin_hbm, cw.at[:, shard_cols(d)], load_sem.at[4]),
    ]
    small = [
        pltpu.make_async_copy(src, dst, load_sem.at[8 + n])
        for n, (src, dst) in enumerate(
            ((attn_hbm, attn_gain), (ids_hbm, ids), (conv_hbm, conv_gain), (depth_hbm, depth_gain), (dw_hbm, dw))
        )
    ]
    loads[0].start()
    small[0].start()
    small[1].start()
    far, near = 1 - chip // 4, chip // 4
    steps = ((0, far), (0, near), (1, far), (2, far), (1, near), (2, near))
    wq_copies = []
    for slot, (kind, group) in enumerate(steps):
        start = pl.multiple_of(768 * kind + SHARD * group, 128)
        copy = pltpu.make_async_copy(wqkv_hbm.at[:, pl.ds(start, SHARD)], wq.at[slot], wq_sem.at[slot])
        copy.start()
        wq_copies.append(copy)
        if slot == 0:
            loads[1].start()
    for copy in small[2:] + loads[2:]:
        copy.start()

    def remote(src, dst, device, ssem, rsem):
        return pltpu.make_async_remote_copy(
            src_ref=src, dst_ref=dst, send_sem=ssem, recv_sem=rsem, device_id=device, device_id_type=MESH
        )

    loads[0].wait()
    small[0].wait()

    def norm_rows(i, _):
        rows = pl.ds(pl.multiple_of(64 * i, 64), 64)
        normed[rows, :] = norm(xv[rows, :].astype(F32), attn_gain[...]).astype(BF16)
        return _

    lax.fori_loop(0, HERE // 64, norm_rows, 0)

    a_up, a_down, a_far = 2 * zp + yh, 2 * zm + yh, 2 * z2 + yh
    b_here, b_up, b_down, b_far = 2 * z + other, 2 * zp + other, 2 * zm + other, 2 * z2 + other

    def piece(dd, p, of=core):
        return cw.at[pl.ds(pl.multiple_of(768 * of + 384 * p, 384), 384), shard_cols(dd)]

    def third(dd, p, n):
        rows = pl.ds(pl.multiple_of(768 * core + 384 * p + 128 * n, 128), 128)
        return cw.at[rows, shard_cols(dd)]

    def gather(src, dst, device, p, n):
        return remote(src, dst, device, g_send.at[p, n], g_recv.at[p, n])

    def start_all(copies):
        for copy in copies:
            copy.start()

    def gather_wait(ref, p, n):
        remote(ref, ref, up, g_send.at[p, n], g_recv.at[p, n]).wait_recv()

    def to_sibling(dd, p, n):
        return remote(piece(dd, p), piece(dd, p), sibling, s_send.at[p, n], s_recv.at[p, n])

    def from_sibling(dd, n):
        for p in range(2):
            ref = piece(dd, p, 1 - core)
            remote(ref, ref, sibling, s_send.at[p, n], s_recv.at[p, n]).wait_recv()

    def gather_1(p):
        own = cin_hbm.at[pl.ds(pl.multiple_of(768 * core + 384 * p, 384), 384)]
        return [
            gather(own, piece(d, p), down, p, 0),
            gather(own, piece(d, p), across, p, 1),
            gather(own, piece(d, p), up, p, 2),
        ]

    def gather_2(p):
        return [
            gather(piece(a_up, p), piece(a_up, p), down, p, 3),
            gather(piece(a_up, p), piece(a_up, p), across, p, 4),
            gather(piece(b_here, p), piece(b_here, p), up, p, 5),
            to_sibling(a_up, p, 0),
            to_sibling(b_here, p, 1),
            to_sibling(a_down, p, 2),
        ]

    def gather_3(p):
        return [
            gather(third(a_far, p, 0), third(a_far, p, 0), across, p, 6),
            gather(third(b_up, p, 1), third(b_up, p, 1), down, p, 7),
            gather(third(b_down, p, 2), third(b_down, p, 2), up, p, 8),
            to_sibling(a_far, p, 3),
            to_sibling(b_up, p, 4),
            to_sibling(b_down, p, 5),
        ]

    def gather_4(p):
        return [to_sibling(b_far, p, 6)]

    def run_2(p):
        gather_wait(piece(a_up, p), p, 0)
        gather_wait(piece(b_here, p), p, 1)
        gather_wait(piece(a_down, p), p, 2)
        start_all(gather_2(p))

    def run_3(p):
        gather_wait(piece(a_far, p), p, 3)
        gather_wait(piece(b_up, p), p, 4)
        gather_wait(piece(b_down, p), p, 5)
        start_all(gather_3(p))

    def run_4(p):
        for n in range(3):
            gather_wait(third(b_far, p, n), p, 6 + n)
        start_all(gather_4(p))

    small[1].wait()
    place = []
    for t in range(2):
        mine = ids[0, 2 * c + t]
        earlier = jnp.int32(0)
        for j in range(BLOCKS):
            earlier = earlier + (ids[0, j] < mine).astype(jnp.int32)
        place.append(lax.min(2 * c + t - earlier, LONG - 1))
    loads[1].wait()
    cosine = jnp.concatenate([tab[place[0], 0], tab[place[1], 0]], axis=1)
    sine = jnp.concatenate([tab[place[0], 1], tab[place[1], 1]], axis=1)
    scale = math.log2(math.e) / math.sqrt(HEAD_DIM)

    def q_slot(i):
        return qbuf.at[i, pl.ds(0, HEAD_DIM)]

    def kv_slot(i, of):
        return kvbuf.at[i, :, pl.ds(0, HEAD_DIM), pl.ds(pl.multiple_of(HERE * of, HERE), HERE)]

    sends = []
    for slot, (kind, group) in enumerate(steps):
        wq_copies[slot].wait()
        turned = jnp.transpose(jnp.dot(normed[...], wq[slot], preferred_element_type=F32))
        for i in range(4):
            first = turned[96 * i : 96 * i + 48]
            second = turned[96 * i + 48 : 96 * i + 96]
            if kind < 2:
                first, second = first * cosine - second * sine, second * cosine + first * sine
            if kind == 0:
                sq[4 * group + i, 0:48, :] = (first * scale).astype(BF16)
                sq[4 * group + i, 48:96, :] = (second * scale).astype(BF16)
            else:
                skv[4 * group + i, kind - 1, 0:48, :] = first.astype(BF16)
                skv[4 * group + i, kind - 1, 48:96, :] = second.astype(BF16)
        if slot == 1:
            pl.semaphore_wait(barrier, len(greeted))
            for off in range(1, 8):
                to = flip(chip, off)
                sends.append(remote(sq.at[to], q_slot(chip), peer(off), q_send.at[off], q_recv.at[off]))
                sends[-1].start()
            start_all(gather_1(0))
            start_all(gather_1(1))
        if slot in (3, 5):
            for off in (range(4, 8) if slot == 3 else range(1, 4)):
                to = flip(chip, off)
                sends.append(remote(skv.at[to], kv_slot(chip, core), peer(off), kv_send.at[off], kv_recv.at[off]))
                sends[-1].start()
    keep_q = pltpu.make_async_copy(sq.at[chip], q_slot(chip), load_sem.at[5])
    keep_kv = pltpu.make_async_copy(skv.at[chip], kv_slot(chip, core), load_sem.at[6])
    keep_q.start()
    keep_kv.start()

    def forward(off, src):
        return remote(src, kv_slot(flip(chip, off), core), sibling, fwd_send.at[off], fwd_recv.at[off])

    forward(0, skv.at[chip]).start()

    row = lax.broadcasted_iota(jnp.int32, (BLOCK - HEAD_DIM, BLOCK), 0)

    def mark_keys(j, _):
        spot = pl.ds(pl.multiple_of(BLOCK * (j % 4), BLOCK), BLOCK)
        kvbuf[j // 4, 0, HEAD_DIM:, spot] = jnp.where(row == ids[0, j], 1.0, 0.0).astype(BF16)
        kvbuf[j // 4, 1, HEAD_DIM:, spot] = jnp.ones((BLOCK - HEAD_DIM, BLOCK), BF16)
        return _

    def mark_queries(j, _):
        spot = pl.ds(pl.multiple_of(BLOCK * (j % 2), BLOCK), BLOCK)
        mine = ids[0, 4 * (j // 2) + 2 * core + j % 2]
        qbuf[j // 2, HEAD_DIM:, spot] = jnp.where(row == mine, 0.0, AWAY).astype(BF16)
        return _

    lax.fori_loop(0, BLOCKS, mark_keys, 0)
    lax.fori_loop(0, 16, mark_queries, 0)
    peaks[...] = jnp.full(peaks.shape, -3e38, F32)
    totals[...] = jnp.zeros(totals.shape, F32)

    keep_q.wait()
    for off in range(1, 8):
        slot = q_slot(flip(chip, off))
        remote(slot, slot, peer(off), q_send.at[off], q_recv.at[off]).wait_recv()
    keep_kv.wait()

    def order(n):
        return lax.select(n < 5, n + 3, n - 4)

    def arrive(off):
        slot = kv_slot(flip(chip, off), core)
        remote(slot, slot, peer(off), kv_send.at[off], kv_recv.at[off]).wait_recv()
        forward(off, slot).start()

    def keys_of(off):
        source = flip(chip, off)
        slot = kv_slot(source, 1 - core)
        remote(slot, slot, sibling, fwd_send.at[off], fwd_recv.at[off]).wait_recv()
        kn[...] = jnp.transpose(kvbuf[source, 0])
        return source

    def attend(source, tiles, last=False):
        scores = [jnp.dot(kn[...], qbuf[i], preferred_element_type=F32) for i in tiles]
        results = []
        for i, score in zip(tiles, scores):
            old = peaks[i]
            top = jnp.maximum(old, jnp.max(score, axis=0, keepdims=True))
            if not last:
                peaks[i] = top
            weights = jnp.exp2(score - top).astype(BF16)
            fresh = jnp.dot(kvbuf[source, 1, 0:112, :], weights, preferred_element_type=F32)
            results.append(totals[i] * jnp.exp2(old - top) + fresh)
        return results

    def use_source(n, _):
        arrive(order(n + 1))
        pl.when(n == 2)(lambda: run_2(0))
        pl.when(n == 5)(lambda: run_2(1))
        source = keys_of(lax.select(n == 0, 0, order(n)))
        for i, total in enumerate(attend(source, range(8))):
            totals[i] = total
        return _

    lax.fori_loop(0, 7, use_source, 0)
    source = keys_of(order(7))

    def o_copy(i, off):
        return remote(osend.at[i], att.at[chip], (d, 2 * i + core), o_send.at[off], o_recv.at[off])

    for offs in ((6, 7, 4, 5), (2, 3, 1, 0)):
        tiles = [flip(chip, off) for off in offs]
        for off, i, total in zip(offs, tiles, attend(source, tiles, last=True)):
            osend[i] = (total[0:96] / total[96:97]).astype(BF16)
            if off:
                o_copy(i, off).start()
    o_keep = pltpu.make_async_copy(osend.at[chip], att.at[chip], load_sem.at[7])
    o_keep.start()

    run_3(0)
    loads[2].wait()
    o_keep.wait()
    for off in range(1, 8):
        slot = att.at[flip(chip, off)]
        remote(slot, slot, peer(off), o_send.at[off], o_recv.at[off]).wait_recv()
    normed[:, 0:768] = jnp.transpose(att[...].reshape(768, HERE))

    def add_out(i, _):
        cols = pl.ds(pl.multiple_of(512 * i, 512), 512)
        resid[:, cols] = xv[:, cols].astype(F32) + jnp.dot(
            normed[:, 0:768], wo[:, cols], preferred_element_type=F32
        )
        return _

    lax.fori_loop(0, 3, add_out, 0)
    run_3(1)

    small[2].wait()

    def norm_residual(i, _):
        rows = pl.ds(pl.multiple_of(64 * i, 64), 64)
        normed[rows, :] = norm(resid[rows, :], conv_gain[...]).astype(BF16)
        return _

    lax.fori_loop(0, HERE // 64, norm_residual, 0)

    def edge_copies(n, v):
        cols = pl.ds(pl.multiple_of(SHARD * v, 128), SHARD)
        return [
            remote(ext.at[pl.ds(256, 16), cols], ext.at[pl.ds(0, 16), cols], right, h_send.at[0, n], h_recv.at[0, n]),
            remote(ext.at[pl.ds(16, 16), cols], ext.at[pl.ds(272, 16), cols], left, h_send.at[1, n], h_recv.at[1, n]),
        ]

    edges = []

    def gate(n, v):
        cols = pl.ds(pl.multiple_of(SHARD * v, 128), SHARD)
        both = pl.ds(pl.multiple_of(2 * SHARD * v, 256), 2 * SHARD)
        wide = jnp.dot(normed[...], cw[:, both], preferred_element_type=F32)
        ext[16:272, cols] = (wide[:, :SHARD] * jax.nn.sigmoid(wide[:, SHARD:])).astype(BF16)
        for copy in edge_copies(n, v):
            copy.start()
            edges.append(copy)

    here_0, here_1 = ids[0, 2 * c], ids[0, 2 * c + 1]
    before = ids[0, lax.max(2 * c - 1, 0)]
    after = ids[0, lax.min(2 * c + 2, BLOCKS - 1)]
    inner = here_0 == here_1
    keeps = (
        (jnp.logical_and(c > 0, before == here_0), inner),
        (inner, jnp.logical_and(c < 15, after == here_1)),
    )

    def taps(n, v):
        for copy in edge_copies(n, v):
            copy.wait_recv()

        def filter_lanes(i, _):
            cols = pl.ds(pl.multiple_of(SHARD * v + BLOCK * i, BLOCK), BLOCK)
            for t in range(2):
                head = ext[BLOCK * t : BLOCK * t + 16, cols].astype(F32)
                tail = ext[BLOCK * t + 144 : BLOCK * t + 160, cols].astype(F32)
                tmp[t, 0:16, :] = jnp.where(keeps[t][0], head, 0.0)
                tmp[t, 16:144, :] = ext[BLOCK * t + 16 : BLOCK * t + 144, cols].astype(F32)
                tmp[t, 144:160, :] = jnp.where(keeps[t][1], tail, 0.0)
                total = jnp.zeros((BLOCK, BLOCK), F32)
                for tap in range(KERNEL):
                    total += dw[tap : tap + 1, cols] * tmp[t, tap + 1 : tap + 1 + BLOCK, :]
                filt[BLOCK * t : BLOCK * t + BLOCK, cols] = total
            return _

        lax.fori_loop(0, 3, filter_lanes, 0)

    groups = (a_up % 4, b_up % 4, d % 4, b_here % 4)
    for n in (0, 2):
        from_sibling((a_up, 0, a_down)[n], n)
    gate(0, groups[0])
    small[3].wait()
    small[4].wait()
    for n, dd in ((4, b_up), (5, b_down)):
        from_sibling(dd, n)
    gate(1, groups[1])
    run_4(0)
    loads[4].wait()
    from_sibling(a_far, 3)
    gate(2, groups[2])
    run_4(1)
    taps(0, groups[0])
    for n, dd in ((1, b_here), (6, b_far)):
        from_sibling(dd, n)
    gate(3, groups[3])
    for n in range(1, 4):
        taps(n, groups[n])

    def norm_filtered(i, _):
        rows = pl.ds(pl.multiple_of(64 * i, 64), 64)
        values = norm(filt[rows, :], depth_gain[...])
        normed[rows, :] = (values / (1.0 + jnp.exp(-values))).astype(BF16)
        return _

    lax.fori_loop(0, HERE // 64, norm_filtered, 0)

    loads[3].wait()

    def out_copy(i):
        cols = pl.ds(pl.multiple_of(512 * i, 512), 512)
        return pltpu.make_async_copy(out.at[:, cols], out_hbm.at[0, :, cols], load_sem.at[13 + i])

    def add_conv(i, _):
        cols = pl.ds(pl.multiple_of(512 * i, 512), 512)
        out[:, cols] = (
            resid[:, cols] + jnp.dot(normed[...], co[:, cols], preferred_element_type=F32)
        ).astype(BF16)
        out_copy(i).start()
        return _

    lax.fori_loop(0, 3, add_conv, 0)

    gathers = [copy for p in range(2) for step in (gather_1, gather_2, gather_3, gather_4) for copy in step(p)]
    for copy in gathers + sends + edges:
        copy.wait_send()
    forward(0, skv.at[chip]).wait_send()

    def drain(off, _):
        forward(off, kv_slot(flip(chip, off), core)).wait_send()
        o_copy(flip(chip, off), off).wait_send()
        return _

    lax.fori_loop(1, 8, drain, 0)
    for i in range(3):
        out_copy(i).wait()


def local(inputs, block_ids, attn_gain, w_qkv, w_out, conv_gain, conv_in, depthwise_w, depth_gain, conv_out):
    in_hbm = pl.BlockSpec(memory_space=pl.ANY)
    dma = pltpu.SemaphoreType.DMA
    return pl.pallas_call(
        kernel,
        out_shape=jax.ShapeDtypeStruct((1, HERE, MODEL_DIM), BF16),
        in_specs=[in_hbm] * 11,
        out_specs=in_hbm,
        scratch_shapes=[
            pltpu.SMEM((1, BLOCKS), jnp.int32),
            pltpu.VMEM((MODEL_DIM,), F32),
            pltpu.VMEM((MODEL_DIM,), F32),
            pltpu.VMEM((MODEL_DIM,), F32),
            pltpu.VMEM((KERNEL, MODEL_DIM), F32),
            pltpu.VMEM((HERE, MODEL_DIM), BF16),
            pltpu.VMEM((HERE, MODEL_DIM), BF16),
            pltpu.VMEM((6, MODEL_DIM, SHARD), BF16),
            pltpu.VMEM((768, MODEL_DIM), BF16),
            pltpu.VMEM((MODEL_DIM, 2 * MODEL_DIM), BF16),
            pltpu.VMEM((MODEL_DIM, MODEL_DIM), BF16),
            pltpu.VMEM((LONG, 2, HALF, BLOCK), F32),
            pltpu.VMEM((HERE, MODEL_DIM), BF16),
            pltpu.VMEM((8, HEAD_DIM, HERE), BF16),
            pltpu.VMEM((8, 2, HEAD_DIM, HERE), BF16),
            pltpu.VMEM((8, BLOCK, HERE), BF16),
            pltpu.VMEM((8, 2, BLOCK, 2 * HERE), BF16),
            pltpu.VMEM((2 * HERE, BLOCK), BF16),
            pltpu.VMEM((8, 1, HERE), F32),
            pltpu.VMEM((8, 112, HERE), F32),
            pltpu.VMEM((8, HEAD_DIM, HERE), BF16),
            pltpu.VMEM((8, HEAD_DIM, HERE), BF16),
            pltpu.VMEM((HERE, MODEL_DIM), F32),
            pltpu.VMEM((HERE, MODEL_DIM), F32),
            pltpu.VMEM((HERE + 32, MODEL_DIM), BF16),
            pltpu.VMEM((2, 160, BLOCK), F32),
            dma((16,)), dma((6,)), dma((8,)), dma((8,)), dma((8,)), dma((8,)), dma((8,)), dma((8,)), dma((8,)), dma((8,)),
            dma((2, 9)), dma((2, 9)), dma((2, 7)), dma((2, 7)), dma((2, 4)), dma((2, 4)),
        ],
        compiler_params=pltpu.CompilerParams(
            collective_id=0, has_side_effects=True, vmem_limit_bytes=56 * 1024 * 1024
        ),
        name="conformer",
    )(
        inputs, block_ids, attn_gain, w_qkv, w_out, conv_gain, conv_in, depthwise_w,
        depth_gain, conv_out, jnp.asarray(rotation_tables()),
    )


def solution(mesh):
    return jax.shard_map(
        local,
        mesh=mesh,
        in_specs=(
            P("dp", "ctx", None),
            P("dp", None),
            P(),
            P(),
            P(),
            P(),
            P(None, "dp"),
            P(),
            P(),
            P(),
        ),
        out_specs=P("dp", "ctx", None),
        check_vma=False,
    )
```

```python
import functools
import math

import jax
import jax.numpy as jnp
import numpy as np
from jax import lax
from jax.experimental import pallas as pl
from jax.experimental.pallas import tpu as pltpu
from jax.sharding import PartitionSpec as P

MODEL_DIM = 1536
HEAD_COUNT = 8
HEAD_DIM = 96
HALF = HEAD_DIM // 2
KERNEL = 31
BLOCK = 128
BLOCKS = 32
LONG = 24
AWAY = -1e30
HERE = 256
SHARD = 384
EPSILON = 1e-05
MESH = pl.DeviceIdType.MESH
F32 = jnp.float32
BF16 = jnp.bfloat16


def rotation_tables():
    inverse = 10000.0 ** (-np.arange(HALF, dtype=np.float64) / HALF)
    angles = np.arange(LONG * BLOCK, dtype=np.float64)[None, :] * inverse[:, None]
    pair = np.stack([np.cos(angles), np.sin(angles)])
    pair = pair.reshape(2, HALF, LONG, BLOCK).transpose(2, 0, 1, 3)
    return np.ascontiguousarray(pair).astype(np.float32)


def norm(values, gain):
    average = jnp.mean(values, axis=-1, keepdims=True)
    centred = values - average
    variance = jnp.mean(centred * centred, axis=-1, keepdims=True)
    return centred * lax.rsqrt(variance + EPSILON) * gain


def flip(index, off):
    out = index
    for bit in (1, 2, 4):
        out = out + bit * ((off // bit) % 2) * (1 - 2 * ((index // bit) % 2))
    return out


def kernel(
    x_hbm, ids_hbm, attn_hbm, wqkv_hbm, wout_hbm, conv_hbm, cin_hbm, dw_hbm, depth_hbm, cout_hbm, tab_hbm,
    out_hbm,
    ids, attn_gain, conv_gain, depth_gain, dw, out, xv, wq, wo, cw, co, tab, normed, sq, skv, qbuf, kvbuf, kn, peaks, totals, osend, att, resid, filt, ext, tmp,
    load_sem, wq_sem, q_send, q_recv, kv_send, kv_recv, fwd_send, fwd_recv, o_send, o_recv,
    g_send, g_recv, s_send, s_recv, h_send, h_recv,
):
    d = lax.axis_index("dp")
    c = lax.axis_index("ctx")
    chip, core = c // 2, c % 2
    sibling = (d, c + 1 - 2 * core)
    z, yh = d // 2, d % 2
    zp, zm, z2 = (z + 1) % 4, (z + 3) % 4, (z + 2) % 4
    other = 1 - yh
    across = (2 * z + other, c + 2 - 4 * (chip % 2))
    up, down = (2 * zp + yh, c), (2 * zm + yh, c)
    right, left = (d, (c + 1) % 16), (d, (c + 15) % 16)

    def peer(off):
        return (d, 2 * flip(chip, off) + core)

    barrier = pltpu.get_barrier_semaphore()
    cross = (d, lax.select(core == 0, (c + 15) % 16, (c + 1) % 16))
    greeted = [peer(off) for off in range(1, 8)] + [sibling, across, up, down, cross]
    for device in greeted:
        pl.semaphore_signal(barrier, inc=1, device_id=device, device_id_type=MESH)

    def shard_cols(dd):
        return pl.ds(pl.multiple_of(SHARD * (2 * (dd % 4) + dd // 4), 128), SHARD)

    loads = [
        pltpu.make_async_copy(x_hbm.at[0], xv, load_sem.at[0]),
        pltpu.make_async_copy(tab_hbm, tab, load_sem.at[1]),
        pltpu.make_async_copy(wout_hbm, wo, load_sem.at[2]),
        pltpu.make_async_copy(cout_hbm, co, load_sem.at[3]),
        pltpu.make_async_copy(cin_hbm, cw.at[:, shard_cols(d)], load_sem.at[4]),
    ]
    small = [
        pltpu.make_async_copy(src, dst, load_sem.at[8 + n])
        for n, (src, dst) in enumerate(
            ((attn_hbm, attn_gain), (ids_hbm, ids), (conv_hbm, conv_gain), (depth_hbm, depth_gain), (dw_hbm, dw))
        )
    ]
    loads[0].start()
    small[0].start()
    small[1].start()
    far, near = 1 - chip // 4, chip // 4
    steps = ((0, far), (0, near), (1, far), (2, far), (1, near), (2, near))
    wq_copies = []
    for slot, (kind, group) in enumerate(steps):
        start = pl.multiple_of(768 * kind + SHARD * group, 128)
        copy = pltpu.make_async_copy(wqkv_hbm.at[:, pl.ds(start, SHARD)], wq.at[slot], wq_sem.at[slot])
        copy.start()
        wq_copies.append(copy)
        if slot == 0:
            loads[1].start()
    for copy in small[2:] + loads[2:]:
        copy.start()

    def remote(src, dst, device, ssem, rsem):
        return pltpu.make_async_remote_copy(
            src_ref=src, dst_ref=dst, send_sem=ssem, recv_sem=rsem, device_id=device, device_id_type=MESH
        )

    loads[0].wait()
    small[0].wait()

    def norm_rows(i, _):
        rows = pl.ds(pl.multiple_of(128 * i, 128), 128)
        normed[rows, :] = norm(xv[rows, :].astype(F32), attn_gain[...]).astype(BF16)
        return _

    lax.fori_loop(0, HERE // 128, norm_rows, 0)

    a_up, a_down, a_far = 2 * zp + yh, 2 * zm + yh, 2 * z2 + yh
    b_here, b_up, b_down, b_far = 2 * z + other, 2 * zp + other, 2 * zm + other, 2 * z2 + other

    def piece(dd, p, of=core):
        return cw.at[pl.ds(pl.multiple_of(768 * of + 384 * p, 384), 384), shard_cols(dd)]

    def third(dd, p, n):
        rows = pl.ds(pl.multiple_of(768 * core + 384 * p + 128 * n, 128), 128)
        return cw.at[rows, shard_cols(dd)]

    def gather(src, dst, device, p, n):
        return remote(src, dst, device, g_send.at[p, n], g_recv.at[p, n])

    def start_all(copies):
        for copy in copies:
            copy.start()

    def gather_wait(ref, p, n):
        remote(ref, ref, up, g_send.at[p, n], g_recv.at[p, n]).wait_recv()

    def to_sibling(dd, p, n):
        return remote(piece(dd, p), piece(dd, p), sibling, s_send.at[p, n], s_recv.at[p, n])

    def from_sibling(dd, n):
        for p in range(2):
            ref = piece(dd, p, 1 - core)
            remote(ref, ref, sibling, s_send.at[p, n], s_recv.at[p, n]).wait_recv()

    def gather_1(p):
        own = cin_hbm.at[pl.ds(pl.multiple_of(768 * core + 384 * p, 384), 384)]
        return [
            gather(own, piece(d, p), down, p, 0),
            gather(own, piece(d, p), across, p, 1),
            gather(own, piece(d, p), up, p, 2),
        ]

    def gather_2(p):
        return [
            gather(piece(a_up, p), piece(a_up, p), down, p, 3),
            gather(piece(a_up, p), piece(a_up, p), across, p, 4),
            gather(piece(b_here, p), piece(b_here, p), up, p, 5),
            to_sibling(a_up, p, 0),
            to_sibling(b_here, p, 1),
            to_sibling(a_down, p, 2),
        ]

    def gather_3(p):
        return [
            gather(third(a_far, p, 0), third(a_far, p, 0), across, p, 6),
            gather(third(b_up, p, 1), third(b_up, p, 1), down, p, 7),
            gather(third(b_down, p, 2), third(b_down, p, 2), up, p, 8),
            to_sibling(a_far, p, 3),
            to_sibling(b_up, p, 4),
            to_sibling(b_down, p, 5),
        ]

    def gather_4(p):
        return [to_sibling(b_far, p, 6)]

    def run_2(p):
        gather_wait(piece(a_up, p), p, 0)
        gather_wait(piece(b_here, p), p, 1)
        gather_wait(piece(a_down, p), p, 2)
        start_all(gather_2(p))

    def run_3(p):
        gather_wait(piece(a_far, p), p, 3)
        gather_wait(piece(b_up, p), p, 4)
        gather_wait(piece(b_down, p), p, 5)
        start_all(gather_3(p))

    def run_4(p):
        for n in range(3):
            gather_wait(third(b_far, p, n), p, 6 + n)
        start_all(gather_4(p))

    small[1].wait()
    place = []
    for t in range(2):
        mine = ids[0, 2 * c + t]
        earlier = jnp.int32(0)
        for j in range(BLOCKS):
            earlier = earlier + (ids[0, j] < mine).astype(jnp.int32)
        place.append(lax.min(2 * c + t - earlier, LONG - 1))
    loads[1].wait()
    cosine = jnp.concatenate([tab[place[0], 0], tab[place[1], 0]], axis=1)
    sine = jnp.concatenate([tab[place[0], 1], tab[place[1], 1]], axis=1)
    scale = math.log2(math.e) / math.sqrt(HEAD_DIM)

    def q_slot(i):
        return qbuf.at[i, pl.ds(0, HEAD_DIM)]

    def kv_slot(i, of):
        return kvbuf.at[i, :, pl.ds(0, HEAD_DIM), pl.ds(pl.multiple_of(HERE * of, HERE), HERE)]

    sends = []
    for slot, (kind, group) in enumerate(steps):
        wq_copies[slot].wait()
        turned = jnp.transpose(jnp.dot(normed[...], wq[slot], preferred_element_type=F32))
        for i in range(4):
            first = turned[96 * i : 96 * i + 48]
            second = turned[96 * i + 48 : 96 * i + 96]
            if kind < 2:
                first, second = first * cosine - second * sine, second * cosine + first * sine
            if kind == 0:
                sq[4 * group + i, 0:48, :] = (first * scale).astype(BF16)
                sq[4 * group + i, 48:96, :] = (second * scale).astype(BF16)
            else:
                skv[4 * group + i, kind - 1, 0:48, :] = first.astype(BF16)
                skv[4 * group + i, kind - 1, 48:96, :] = second.astype(BF16)
        if slot == 1:
            pl.semaphore_wait(barrier, len(greeted))
            for off in range(1, 8):
                to = flip(chip, off)
                sends.append(remote(sq.at[to], q_slot(chip), peer(off), q_send.at[off], q_recv.at[off]))
                sends[-1].start()
            start_all(gather_1(0))
            start_all(gather_1(1))
        if slot in (3, 5):
            for off in (range(4, 8) if slot == 3 else range(1, 4)):
                to = flip(chip, off)
                sends.append(remote(skv.at[to], kv_slot(chip, core), peer(off), kv_send.at[off], kv_recv.at[off]))
                sends[-1].start()
    keep_q = pltpu.make_async_copy(sq.at[chip], q_slot(chip), load_sem.at[5])
    keep_kv = pltpu.make_async_copy(skv.at[chip], kv_slot(chip, core), load_sem.at[6])
    keep_q.start()
    keep_kv.start()

    def forward(off, src):
        return remote(src, kv_slot(flip(chip, off), core), sibling, fwd_send.at[off], fwd_recv.at[off])

    forward(0, skv.at[chip]).start()

    row = lax.broadcasted_iota(jnp.int32, (BLOCK - HEAD_DIM, BLOCK), 0)

    def mark_keys(j, _):
        spot = pl.ds(pl.multiple_of(BLOCK * (j % 4), BLOCK), BLOCK)
        kvbuf[j // 4, 0, HEAD_DIM:, spot] = jnp.where(row == ids[0, j], 1.0, 0.0).astype(BF16)
        kvbuf[j // 4, 1, HEAD_DIM:, spot] = jnp.ones((BLOCK - HEAD_DIM, BLOCK), BF16)
        return _

    def mark_queries(j, _):
        spot = pl.ds(pl.multiple_of(BLOCK * (j % 2), BLOCK), BLOCK)
        mine = ids[0, 4 * (j // 2) + 2 * core + j % 2]
        qbuf[j // 2, HEAD_DIM:, spot] = jnp.where(row == mine, 0.0, AWAY).astype(BF16)
        return _

    lax.fori_loop(0, BLOCKS, mark_keys, 0)
    lax.fori_loop(0, 16, mark_queries, 0)
    peaks[...] = jnp.full(peaks.shape, -3e38, F32)
    totals[...] = jnp.zeros(totals.shape, F32)

    keep_q.wait()
    for off in range(1, 8):
        slot = q_slot(flip(chip, off))
        remote(slot, slot, peer(off), q_send.at[off], q_recv.at[off]).wait_recv()
    keep_kv.wait()

    def order(n):
        return lax.select(n < 5, n + 3, n - 4)

    def arrive(off):
        slot = kv_slot(flip(chip, off), core)
        remote(slot, slot, peer(off), kv_send.at[off], kv_recv.at[off]).wait_recv()
        forward(off, slot).start()

    def keys_of(off):
        source = flip(chip, off)
        slot = kv_slot(source, 1 - core)
        remote(slot, slot, sibling, fwd_send.at[off], fwd_recv.at[off]).wait_recv()
        kn[...] = jnp.transpose(kvbuf[source, 0])
        return source

    def attend(source, tiles, last=False):
        scores = [jnp.dot(kn[...], qbuf[i], preferred_element_type=F32) for i in tiles]
        results = []
        for i, score in zip(tiles, scores):
            old = peaks[i]
            top = jnp.maximum(old, jnp.max(score, axis=0, keepdims=True))
            if not last:
                peaks[i] = top
            weights = jnp.exp2(score - top).astype(BF16)
            fresh = jnp.dot(kvbuf[source, 1, 0:112, :], weights, preferred_element_type=F32)
            results.append(totals[i] * jnp.exp2(old - top) + fresh)
        return results

    def use_source(n, _):
        arrive(order(n + 1))
        pl.when(n == 2)(lambda: run_2(0))
        pl.when(n == 5)(lambda: run_2(1))
        source = keys_of(lax.select(n == 0, 0, order(n)))
        for i, total in enumerate(attend(source, range(8))):
            totals[i] = total
        return _

    lax.fori_loop(0, 7, use_source, 0)
    source = keys_of(order(7))

    def o_copy(i, off):
        return remote(osend.at[i], att.at[chip], (d, 2 * i + core), o_send.at[off], o_recv.at[off])

    for offs in ((6, 7, 4, 5), (2, 3, 1, 0)):
        tiles = [flip(chip, off) for off in offs]
        for off, i, total in zip(offs, tiles, attend(source, tiles, last=True)):
            osend[i] = (total[0:96] / total[96:97]).astype(BF16)
            if off:
                o_copy(i, off).start()
    o_keep = pltpu.make_async_copy(osend.at[chip], att.at[chip], load_sem.at[7])
    o_keep.start()

    run_3(0)
    loads[2].wait()
    o_keep.wait()
    for off in range(1, 8):
        slot = att.at[flip(chip, off)]
        remote(slot, slot, peer(off), o_send.at[off], o_recv.at[off]).wait_recv()
    normed[:, 0:768] = jnp.transpose(att[...].reshape(768, HERE))

    def add_out(i, _):
        cols = pl.ds(pl.multiple_of(512 * i, 512), 512)
        resid[:, cols] = xv[:, cols].astype(F32) + jnp.dot(
            normed[:, 0:768], wo[:, cols], preferred_element_type=F32
        )
        return _

    lax.fori_loop(0, 3, add_out, 0)
    run_3(1)

    small[2].wait()

    def norm_residual(i, _):
        rows = pl.ds(pl.multiple_of(128 * i, 128), 128)
        normed[rows, :] = norm(resid[rows, :], conv_gain[...]).astype(BF16)
        return _

    lax.fori_loop(0, HERE // 128, norm_residual, 0)

    def edge_copies(n, v):
        cols = pl.ds(pl.multiple_of(SHARD * v, 128), SHARD)
        return [
            remote(ext.at[pl.ds(256, 16), cols], ext.at[pl.ds(0, 16), cols], right, h_send.at[0, n], h_recv.at[0, n]),
            remote(ext.at[pl.ds(16, 16), cols], ext.at[pl.ds(272, 16), cols], left, h_send.at[1, n], h_recv.at[1, n]),
        ]

    edges = []

    def gate(n, v):
        cols = pl.ds(pl.multiple_of(SHARD * v, 128), SHARD)
        both = pl.ds(pl.multiple_of(2 * SHARD * v, 256), 2 * SHARD)
        wide = jnp.dot(normed[...], cw[:, both], preferred_element_type=F32)
        ext[16:272, cols] = (wide[:, :SHARD] * jax.nn.sigmoid(wide[:, SHARD:])).astype(BF16)
        for copy in edge_copies(n, v):
            copy.start()
            edges.append(copy)

    here_0, here_1 = ids[0, 2 * c], ids[0, 2 * c + 1]
    before = ids[0, lax.max(2 * c - 1, 0)]
    after = ids[0, lax.min(2 * c + 2, BLOCKS - 1)]
    inner = here_0 == here_1
    keeps = (
        (jnp.logical_and(c > 0, before == here_0), inner),
        (inner, jnp.logical_and(c < 15, after == here_1)),
    )

    def taps(n, v):
        for copy in edge_copies(n, v):
            copy.wait_recv()

        def filter_lanes(i, _):
            cols = pl.ds(pl.multiple_of(SHARD * v + BLOCK * i, BLOCK), BLOCK)
            for t in range(2):
                head = ext[BLOCK * t : BLOCK * t + 16, cols].astype(F32)
                tail = ext[BLOCK * t + 144 : BLOCK * t + 160, cols].astype(F32)
                tmp[t, 0:16, :] = jnp.where(keeps[t][0], head, 0.0)
                tmp[t, 16:144, :] = ext[BLOCK * t + 16 : BLOCK * t + 144, cols].astype(F32)
                tmp[t, 144:160, :] = jnp.where(keeps[t][1], tail, 0.0)
                total = jnp.zeros((BLOCK, BLOCK), F32)
                for tap in range(KERNEL):
                    total += dw[tap : tap + 1, cols] * tmp[t, tap + 1 : tap + 1 + BLOCK, :]
                filt[BLOCK * t : BLOCK * t + BLOCK, cols] = total
            return _

        lax.fori_loop(0, 3, filter_lanes, 0)

    groups = (a_up % 4, b_up % 4, d % 4, b_here % 4)
    for n in (0, 2):
        from_sibling((a_up, 0, a_down)[n], n)
    gate(0, groups[0])
    small[3].wait()
    small[4].wait()
    for n, dd in ((4, b_up), (5, b_down)):
        from_sibling(dd, n)
    gate(1, groups[1])
    run_4(0)
    loads[4].wait()
    from_sibling(a_far, 3)
    gate(2, groups[2])
    run_4(1)
    taps(0, groups[0])
    for n, dd in ((1, b_here), (6, b_far)):
        from_sibling(dd, n)
    gate(3, groups[3])
    for n in range(1, 4):
        taps(n, groups[n])

    def norm_filtered(i, _):
        rows = pl.ds(pl.multiple_of(128 * i, 128), 128)
        values = norm(filt[rows, :], depth_gain[...])
        normed[rows, :] = (values / (1.0 + jnp.exp(-values))).astype(BF16)
        return _

    lax.fori_loop(0, HERE // 128, norm_filtered, 0)

    loads[3].wait()

    def out_copy(i):
        cols = pl.ds(pl.multiple_of(512 * i, 512), 512)
        return pltpu.make_async_copy(out.at[:, cols], out_hbm.at[0, :, cols], load_sem.at[13 + i])

    def add_conv(i, _):
        cols = pl.ds(pl.multiple_of(512 * i, 512), 512)
        out[:, cols] = (
            resid[:, cols] + jnp.dot(normed[...], co[:, cols], preferred_element_type=F32)
        ).astype(BF16)
        out_copy(i).start()
        return _

    lax.fori_loop(0, 3, add_conv, 0)

    gathers = [copy for p in range(2) for step in (gather_1, gather_2, gather_3, gather_4) for copy in step(p)]
    for copy in gathers + sends + edges:
        copy.wait_send()
    forward(0, skv.at[chip]).wait_send()

    def drain(off, _):
        forward(off, kv_slot(flip(chip, off), core)).wait_send()
        o_copy(flip(chip, off), off).wait_send()
        return _

    lax.fori_loop(1, 8, drain, 0)
    for i in range(3):
        out_copy(i).wait()


def local(inputs, block_ids, attn_gain, w_qkv, w_out, conv_gain, conv_in, depthwise_w, depth_gain, conv_out):
    in_hbm = pl.BlockSpec(memory_space=pl.ANY)
    dma = pltpu.SemaphoreType.DMA
    return pl.pallas_call(
        kernel,
        out_shape=jax.ShapeDtypeStruct((1, HERE, MODEL_DIM), BF16),
        in_specs=[in_hbm] * 11,
        out_specs=in_hbm,
        scratch_shapes=[
            pltpu.SMEM((1, BLOCKS), jnp.int32),
            pltpu.VMEM((MODEL_DIM,), F32),
            pltpu.VMEM((MODEL_DIM,), F32),
            pltpu.VMEM((MODEL_DIM,), F32),
            pltpu.VMEM((KERNEL, MODEL_DIM), F32),
            pltpu.VMEM((HERE, MODEL_DIM), BF16),
            pltpu.VMEM((HERE, MODEL_DIM), BF16),
            pltpu.VMEM((6, MODEL_DIM, SHARD), BF16),
            pltpu.VMEM((768, MODEL_DIM), BF16),
            pltpu.VMEM((MODEL_DIM, 2 * MODEL_DIM), BF16),
            pltpu.VMEM((MODEL_DIM, MODEL_DIM), BF16),
            pltpu.VMEM((LONG, 2, HALF, BLOCK), F32),
            pltpu.VMEM((HERE, MODEL_DIM), BF16),
            pltpu.VMEM((8, HEAD_DIM, HERE), BF16),
            pltpu.VMEM((8, 2, HEAD_DIM, HERE), BF16),
            pltpu.VMEM((8, BLOCK, HERE), BF16),
            pltpu.VMEM((8, 2, BLOCK, 2 * HERE), BF16),
            pltpu.VMEM((2 * HERE, BLOCK), BF16),
            pltpu.VMEM((8, 1, HERE), F32),
            pltpu.VMEM((8, 112, HERE), F32),
            pltpu.VMEM((8, HEAD_DIM, HERE), BF16),
            pltpu.VMEM((8, HEAD_DIM, HERE), BF16),
            pltpu.VMEM((HERE, MODEL_DIM), F32),
            pltpu.VMEM((HERE, MODEL_DIM), F32),
            pltpu.VMEM((HERE + 32, MODEL_DIM), BF16),
            pltpu.VMEM((2, 160, BLOCK), F32),
            dma((16,)), dma((6,)), dma((8,)), dma((8,)), dma((8,)), dma((8,)), dma((8,)), dma((8,)), dma((8,)), dma((8,)),
            dma((2, 9)), dma((2, 9)), dma((2, 7)), dma((2, 7)), dma((2, 4)), dma((2, 4)),
        ],
        compiler_params=pltpu.CompilerParams(
            collective_id=0, has_side_effects=True, vmem_limit_bytes=56 * 1024 * 1024
        ),
        name="conformer",
    )(
        inputs, block_ids, attn_gain, w_qkv, w_out, conv_gain, conv_in, depthwise_w,
        depth_gain, conv_out, jnp.asarray(rotation_tables()),
    )


def solution(mesh):
    return jax.shard_map(
        local,
        mesh=mesh,
        in_specs=(
            P("dp", "ctx", None),
            P("dp", None),
            P(),
            P(),
            P(),
            P(),
            P(None, "dp"),
            P(),
            P(),
            P(),
        ),
        out_specs=P("dp", "ctx", None),
        check_vma=False,
    )
```

```python
import functools
import math

import jax
import jax.numpy as jnp
import numpy as np
from jax import lax
from jax.experimental import pallas as pl
from jax.experimental.pallas import tpu as pltpu
from jax.sharding import PartitionSpec as P

MODEL_DIM = 1536
HEAD_COUNT = 8
HEAD_DIM = 96
HALF = HEAD_DIM // 2
KERNEL = 31
BLOCK = 128
BLOCKS = 32
LONG = 24
AWAY = -1e30
HERE = 256
SHARD = 384
EPSILON = 1e-05
MESH = pl.DeviceIdType.MESH
F32 = jnp.float32
BF16 = jnp.bfloat16


def rotation_tables():
    inverse = 10000.0 ** (-np.arange(HALF, dtype=np.float64) / HALF)
    angles = np.arange(LONG * BLOCK, dtype=np.float64)[None, :] * inverse[:, None]
    pair = np.stack([np.cos(angles), np.sin(angles)])
    pair = pair.reshape(2, HALF, LONG, BLOCK).transpose(2, 0, 1, 3)
    return np.ascontiguousarray(pair).astype(np.float32)


def norm(values, gain):
    average = jnp.mean(values, axis=-1, keepdims=True)
    centred = values - average
    variance = jnp.mean(centred * centred, axis=-1, keepdims=True)
    return centred * lax.rsqrt(variance + EPSILON) * gain


def flip(index, off):
    out = index
    for bit in (1, 2, 4):
        out = out + bit * ((off // bit) % 2) * (1 - 2 * ((index // bit) % 2))
    return out


def kernel(
    x_hbm, ids_hbm, attn_hbm, wqkv_hbm, wout_hbm, conv_hbm, cin_hbm, dw_hbm, depth_hbm, cout_hbm, tab_hbm,
    out_hbm,
    ids, attn_gain, conv_gain, depth_gain, dw, out, xv, wq, wo, cw, co, tab, normed, sq, skv, qbuf, kvbuf, kn, peaks, totals, osend, att, resid, filt, ext, tmp,
    load_sem, wq_sem, q_send, q_recv, kv_send, kv_recv, fwd_send, fwd_recv, o_send, o_recv,
    g_send, g_recv, s_send, s_recv, h_send, h_recv,
):
    d = lax.axis_index("dp")
    c = lax.axis_index("ctx")
    chip, core = c // 2, c % 2
    sibling = (d, c + 1 - 2 * core)
    z, yh = d // 2, d % 2
    zp, zm, z2 = (z + 1) % 4, (z + 3) % 4, (z + 2) % 4
    other = 1 - yh
    across = (2 * z + other, c + 2 - 4 * (chip % 2))
    up, down = (2 * zp + yh, c), (2 * zm + yh, c)
    right, left = (d, (c + 1) % 16), (d, (c + 15) % 16)

    def peer(off):
        return (d, 2 * flip(chip, off) + core)

    barrier = pltpu.get_barrier_semaphore()
    cross = (d, lax.select(core == 0, (c + 15) % 16, (c + 1) % 16))
    greeted = [peer(off) for off in range(1, 8)] + [sibling, across, up, down, cross]
    for device in greeted:
        pl.semaphore_signal(barrier, inc=1, device_id=device, device_id_type=MESH)

    def shard_cols(dd):
        return pl.ds(pl.multiple_of(SHARD * (2 * (dd % 4) + dd // 4), 128), SHARD)

    loads = [
        pltpu.make_async_copy(x_hbm.at[0], xv, load_sem.at[0]),
        pltpu.make_async_copy(tab_hbm, tab, load_sem.at[1]),
        pltpu.make_async_copy(wout_hbm, wo, load_sem.at[2]),
        pltpu.make_async_copy(cout_hbm, co, load_sem.at[3]),
        pltpu.make_async_copy(cin_hbm, cw.at[:, shard_cols(d)], load_sem.at[4]),
    ]
    small = [
        pltpu.make_async_copy(src, dst, load_sem.at[8 + n])
        for n, (src, dst) in enumerate(
            ((attn_hbm, attn_gain), (ids_hbm, ids), (conv_hbm, conv_gain), (depth_hbm, depth_gain), (dw_hbm, dw))
        )
    ]
    loads[0].start()
    small[0].start()
    small[1].start()
    far, near = 1 - chip // 4, chip // 4
    steps = ((0, far), (0, near), (1, far), (2, far), (1, near), (2, near))
    wq_copies = []
    for slot, (kind, group) in enumerate(steps):
        start = pl.multiple_of(768 * kind + SHARD * group, 128)
        copy = pltpu.make_async_copy(wqkv_hbm.at[:, pl.ds(start, SHARD)], wq.at[slot], wq_sem.at[slot])
        copy.start()
        wq_copies.append(copy)
        if slot == 0:
            loads[1].start()
    for copy in small[2:] + loads[2:]:
        copy.start()

    def remote(src, dst, device, ssem, rsem):
        return pltpu.make_async_remote_copy(
            src_ref=src, dst_ref=dst, send_sem=ssem, recv_sem=rsem, device_id=device, device_id_type=MESH
        )

    loads[0].wait()
    small[0].wait()

    def norm_rows(i, _):
        rows = pl.ds(pl.multiple_of(256 * i, 256), 256)
        normed[rows, :] = norm(xv[rows, :].astype(F32), attn_gain[...]).astype(BF16)
        return _

    lax.fori_loop(0, HERE // 256, norm_rows, 0)

    a_up, a_down, a_far = 2 * zp + yh, 2 * zm + yh, 2 * z2 + yh
    b_here, b_up, b_down, b_far = 2 * z + other, 2 * zp + other, 2 * zm + other, 2 * z2 + other

    def piece(dd, p, of=core):
        return cw.at[pl.ds(pl.multiple_of(768 * of + 384 * p, 384), 384), shard_cols(dd)]

    def third(dd, p, n):
        rows = pl.ds(pl.multiple_of(768 * core + 384 * p + 128 * n, 128), 128)
        return cw.at[rows, shard_cols(dd)]

    def gather(src, dst, device, p, n):
        return remote(src, dst, device, g_send.at[p, n], g_recv.at[p, n])

    def start_all(copies):
        for copy in copies:
            copy.start()

    def gather_wait(ref, p, n):
        remote(ref, ref, up, g_send.at[p, n], g_recv.at[p, n]).wait_recv()

    def to_sibling(dd, p, n):
        return remote(piece(dd, p), piece(dd, p), sibling, s_send.at[p, n], s_recv.at[p, n])

    def from_sibling(dd, n):
        for p in range(2):
            ref = piece(dd, p, 1 - core)
            remote(ref, ref, sibling, s_send.at[p, n], s_recv.at[p, n]).wait_recv()

    def gather_1(p):
        own = cin_hbm.at[pl.ds(pl.multiple_of(768 * core + 384 * p, 384), 384)]
        return [
            gather(own, piece(d, p), down, p, 0),
            gather(own, piece(d, p), across, p, 1),
            gather(own, piece(d, p), up, p, 2),
        ]

    def gather_2(p):
        return [
            gather(piece(a_up, p), piece(a_up, p), down, p, 3),
            gather(piece(a_up, p), piece(a_up, p), across, p, 4),
            gather(piece(b_here, p), piece(b_here, p), up, p, 5),
            to_sibling(a_up, p, 0),
            to_sibling(b_here, p, 1),
            to_sibling(a_down, p, 2),
        ]

    def gather_3(p):
        return [
            gather(third(a_far, p, 0), third(a_far, p, 0), across, p, 6),
            gather(third(b_up, p, 1), third(b_up, p, 1), down, p, 7),
            gather(third(b_down, p, 2), third(b_down, p, 2), up, p, 8),
            to_sibling(a_far, p, 3),
            to_sibling(b_up, p, 4),
            to_sibling(b_down, p, 5),
        ]

    def gather_4(p):
        return [to_sibling(b_far, p, 6)]

    def run_2(p):
        gather_wait(piece(a_up, p), p, 0)
        gather_wait(piece(b_here, p), p, 1)
        gather_wait(piece(a_down, p), p, 2)
        start_all(gather_2(p))

    def run_3(p):
        gather_wait(piece(a_far, p), p, 3)
        gather_wait(piece(b_up, p), p, 4)
        gather_wait(piece(b_down, p), p, 5)
        start_all(gather_3(p))

    def run_4(p):
        for n in range(3):
            gather_wait(third(b_far, p, n), p, 6 + n)
        start_all(gather_4(p))

    small[1].wait()
    place = []
    for t in range(2):
        mine = ids[0, 2 * c + t]
        earlier = jnp.int32(0)
        for j in range(BLOCKS):
            earlier = earlier + (ids[0, j] < mine).astype(jnp.int32)
        place.append(lax.min(2 * c + t - earlier, LONG - 1))
    loads[1].wait()
    cosine = jnp.concatenate([tab[place[0], 0], tab[place[1], 0]], axis=1)
    sine = jnp.concatenate([tab[place[0], 1], tab[place[1], 1]], axis=1)
    scale = math.log2(math.e) / math.sqrt(HEAD_DIM)

    def q_slot(i):
        return qbuf.at[i, pl.ds(0, HEAD_DIM)]

    def kv_slot(i, of):
        return kvbuf.at[i, :, pl.ds(0, HEAD_DIM), pl.ds(pl.multiple_of(HERE * of, HERE), HERE)]

    sends = []
    for slot, (kind, group) in enumerate(steps):
        wq_copies[slot].wait()
        turned = jnp.transpose(jnp.dot(normed[...], wq[slot], preferred_element_type=F32))
        for i in range(4):
            first = turned[96 * i : 96 * i + 48]
            second = turned[96 * i + 48 : 96 * i + 96]
            if kind < 2:
                first, second = first * cosine - second * sine, second * cosine + first * sine
            if kind == 0:
                sq[4 * group + i, 0:48, :] = (first * scale).astype(BF16)
                sq[4 * group + i, 48:96, :] = (second * scale).astype(BF16)
            else:
                skv[4 * group + i, kind - 1, 0:48, :] = first.astype(BF16)
                skv[4 * group + i, kind - 1, 48:96, :] = second.astype(BF16)
        if slot == 1:
            pl.semaphore_wait(barrier, len(greeted))
            for off in range(1, 8):
                to = flip(chip, off)
                sends.append(remote(sq.at[to], q_slot(chip), peer(off), q_send.at[off], q_recv.at[off]))
                sends[-1].start()
            start_all(gather_1(0))
            start_all(gather_1(1))
        if slot in (3, 5):
            for off in (range(4, 8) if slot == 3 else range(1, 4)):
                to = flip(chip, off)
                sends.append(remote(skv.at[to], kv_slot(chip, core), peer(off), kv_send.at[off], kv_recv.at[off]))
                sends[-1].start()
    keep_q = pltpu.make_async_copy(sq.at[chip], q_slot(chip), load_sem.at[5])
    keep_kv = pltpu.make_async_copy(skv.at[chip], kv_slot(chip, core), load_sem.at[6])
    keep_q.start()
    keep_kv.start()

    def forward(off, src):
        return remote(src, kv_slot(flip(chip, off), core), sibling, fwd_send.at[off], fwd_recv.at[off])

    forward(0, skv.at[chip]).start()

    row = lax.broadcasted_iota(jnp.int32, (BLOCK - HEAD_DIM, BLOCK), 0)

    def mark_keys(j, _):
        spot = pl.ds(pl.multiple_of(BLOCK * (j % 4), BLOCK), BLOCK)
        kvbuf[j // 4, 0, HEAD_DIM:, spot] = jnp.where(row == ids[0, j], 1.0, 0.0).astype(BF16)
        kvbuf[j // 4, 1, HEAD_DIM:, spot] = jnp.ones((BLOCK - HEAD_DIM, BLOCK), BF16)
        return _

    def mark_queries(j, _):
        spot = pl.ds(pl.multiple_of(BLOCK * (j % 2), BLOCK), BLOCK)
        mine = ids[0, 4 * (j // 2) + 2 * core + j % 2]
        qbuf[j // 2, HEAD_DIM:, spot] = jnp.where(row == mine, 0.0, AWAY).astype(BF16)
        return _

    lax.fori_loop(0, BLOCKS, mark_keys, 0)
    lax.fori_loop(0, 16, mark_queries, 0)
    peaks[...] = jnp.full(peaks.shape, -3e38, F32)
    totals[...] = jnp.zeros(totals.shape, F32)

    keep_q.wait()
    for off in range(1, 8):
        slot = q_slot(flip(chip, off))
        remote(slot, slot, peer(off), q_send.at[off], q_recv.at[off]).wait_recv()
    keep_kv.wait()

    def order(n):
        return lax.select(n < 5, n + 3, n - 4)

    def arrive(off):
        slot = kv_slot(flip(chip, off), core)
        remote(slot, slot, peer(off), kv_send.at[off], kv_recv.at[off]).wait_recv()
        forward(off, slot).start()

    def keys_of(off):
        source = flip(chip, off)
        slot = kv_slot(source, 1 - core)
        remote(slot, slot, sibling, fwd_send.at[off], fwd_recv.at[off]).wait_recv()
        kn[...] = jnp.transpose(kvbuf[source, 0])
        return source

    def attend(source, tiles, last=False):
        scores = [jnp.dot(kn[...], qbuf[i], preferred_element_type=F32) for i in tiles]
        results = []
        for i, score in zip(tiles, scores):
            old = peaks[i]
            top = jnp.maximum(old, jnp.max(score, axis=0, keepdims=True))
            if not last:
                peaks[i] = top
            weights = jnp.exp2(score - top).astype(BF16)
            fresh = jnp.dot(kvbuf[source, 1, 0:112, :], weights, preferred_element_type=F32)
            results.append(totals[i] * jnp.exp2(old - top) + fresh)
        return results

    def use_source(n, _):
        arrive(order(n + 1))
        pl.when(n == 2)(lambda: run_2(0))
        pl.when(n == 5)(lambda: run_2(1))
        source = keys_of(lax.select(n == 0, 0, order(n)))
        for i, total in enumerate(attend(source, range(8))):
            totals[i] = total
        return _

    lax.fori_loop(0, 7, use_source, 0)
    source = keys_of(order(7))

    def o_copy(i, off):
        return remote(osend.at[i], att.at[chip], (d, 2 * i + core), o_send.at[off], o_recv.at[off])

    for offs in ((6, 7, 4, 5), (2, 3, 1, 0)):
        tiles = [flip(chip, off) for off in offs]
        for off, i, total in zip(offs, tiles, attend(source, tiles, last=True)):
            osend[i] = (total[0:96] / total[96:97]).astype(BF16)
            if off:
                o_copy(i, off).start()
    o_keep = pltpu.make_async_copy(osend.at[chip], att.at[chip], load_sem.at[7])
    o_keep.start()

    run_3(0)
    loads[2].wait()
    o_keep.wait()
    for off in range(1, 8):
        slot = att.at[flip(chip, off)]
        remote(slot, slot, peer(off), o_send.at[off], o_recv.at[off]).wait_recv()
    normed[:, 0:768] = jnp.transpose(att[...].reshape(768, HERE))

    def add_out(i, _):
        cols = pl.ds(pl.multiple_of(512 * i, 512), 512)
        resid[:, cols] = xv[:, cols].astype(F32) + jnp.dot(
            normed[:, 0:768], wo[:, cols], preferred_element_type=F32
        )
        return _

    lax.fori_loop(0, 3, add_out, 0)
    run_3(1)

    small[2].wait()

    def norm_residual(i, _):
        rows = pl.ds(pl.multiple_of(256 * i, 256), 256)
        normed[rows, :] = norm(resid[rows, :], conv_gain[...]).astype(BF16)
        return _

    lax.fori_loop(0, HERE // 256, norm_residual, 0)

    def edge_copies(n, v):
        cols = pl.ds(pl.multiple_of(SHARD * v, 128), SHARD)
        return [
            remote(ext.at[pl.ds(256, 16), cols], ext.at[pl.ds(0, 16), cols], right, h_send.at[0, n], h_recv.at[0, n]),
            remote(ext.at[pl.ds(16, 16), cols], ext.at[pl.ds(272, 16), cols], left, h_send.at[1, n], h_recv.at[1, n]),
        ]

    edges = []

    def gate(n, v):
        cols = pl.ds(pl.multiple_of(SHARD * v, 128), SHARD)
        both = pl.ds(pl.multiple_of(2 * SHARD * v, 256), 2 * SHARD)
        wide = jnp.dot(normed[...], cw[:, both], preferred_element_type=F32)
        ext[16:272, cols] = (wide[:, :SHARD] * jax.nn.sigmoid(wide[:, SHARD:])).astype(BF16)
        for copy in edge_copies(n, v):
            copy.start()
            edges.append(copy)

    here_0, here_1 = ids[0, 2 * c], ids[0, 2 * c + 1]
    before = ids[0, lax.max(2 * c - 1, 0)]
    after = ids[0, lax.min(2 * c + 2, BLOCKS - 1)]
    inner = here_0 == here_1
    keeps = (
        (jnp.logical_and(c > 0, before == here_0), inner),
        (inner, jnp.logical_and(c < 15, after == here_1)),
    )

    def taps(n, v):
        for copy in edge_copies(n, v):
            copy.wait_recv()

        def filter_lanes(i, _):
            cols = pl.ds(pl.multiple_of(SHARD * v + BLOCK * i, BLOCK), BLOCK)
            for t in range(2):
                head = ext[BLOCK * t : BLOCK * t + 16, cols].astype(F32)
                tail = ext[BLOCK * t + 144 : BLOCK * t + 160, cols].astype(F32)
                tmp[t, 0:16, :] = jnp.where(keeps[t][0], head, 0.0)
                tmp[t, 16:144, :] = ext[BLOCK * t + 16 : BLOCK * t + 144, cols].astype(F32)
                tmp[t, 144:160, :] = jnp.where(keeps[t][1], tail, 0.0)
                total = jnp.zeros((BLOCK, BLOCK), F32)
                for tap in range(KERNEL):
                    total += dw[tap : tap + 1, cols] * tmp[t, tap + 1 : tap + 1 + BLOCK, :]
                filt[BLOCK * t : BLOCK * t + BLOCK, cols] = total
            return _

        lax.fori_loop(0, 3, filter_lanes, 0)

    groups = (a_up % 4, b_up % 4, d % 4, b_here % 4)
    for n in (0, 2):
        from_sibling((a_up, 0, a_down)[n], n)
    gate(0, groups[0])
    small[3].wait()
    small[4].wait()
    for n, dd in ((4, b_up), (5, b_down)):
        from_sibling(dd, n)
    gate(1, groups[1])
    run_4(0)
    loads[4].wait()
    from_sibling(a_far, 3)
    gate(2, groups[2])
    run_4(1)
    taps(0, groups[0])
    for n, dd in ((1, b_here), (6, b_far)):
        from_sibling(dd, n)
    gate(3, groups[3])
    for n in range(1, 4):
        taps(n, groups[n])

    def norm_filtered(i, _):
        rows = pl.ds(pl.multiple_of(256 * i, 256), 256)
        values = norm(filt[rows, :], depth_gain[...])
        normed[rows, :] = (values / (1.0 + jnp.exp(-values))).astype(BF16)
        return _

    lax.fori_loop(0, HERE // 256, norm_filtered, 0)

    loads[3].wait()

    def out_copy(i):
        cols = pl.ds(pl.multiple_of(512 * i, 512), 512)
        return pltpu.make_async_copy(out.at[:, cols], out_hbm.at[0, :, cols], load_sem.at[13 + i])

    def add_conv(i, _):
        cols = pl.ds(pl.multiple_of(512 * i, 512), 512)
        out[:, cols] = (
            resid[:, cols] + jnp.dot(normed[...], co[:, cols], preferred_element_type=F32)
        ).astype(BF16)
        out_copy(i).start()
        return _

    lax.fori_loop(0, 3, add_conv, 0)

    gathers = [copy for p in range(2) for step in (gather_1, gather_2, gather_3, gather_4) for copy in step(p)]
    for copy in gathers + sends + edges:
        copy.wait_send()
    forward(0, skv.at[chip]).wait_send()

    def drain(off, _):
        forward(off, kv_slot(flip(chip, off), core)).wait_send()
        o_copy(flip(chip, off), off).wait_send()
        return _

    lax.fori_loop(1, 8, drain, 0)
    for i in range(3):
        out_copy(i).wait()


def local(inputs, block_ids, attn_gain, w_qkv, w_out, conv_gain, conv_in, depthwise_w, depth_gain, conv_out):
    in_hbm = pl.BlockSpec(memory_space=pl.ANY)
    dma = pltpu.SemaphoreType.DMA
    return pl.pallas_call(
        kernel,
        out_shape=jax.ShapeDtypeStruct((1, HERE, MODEL_DIM), BF16),
        in_specs=[in_hbm] * 11,
        out_specs=in_hbm,
        scratch_shapes=[
            pltpu.SMEM((1, BLOCKS), jnp.int32),
            pltpu.VMEM((MODEL_DIM,), F32),
            pltpu.VMEM((MODEL_DIM,), F32),
            pltpu.VMEM((MODEL_DIM,), F32),
            pltpu.VMEM((KERNEL, MODEL_DIM), F32),
            pltpu.VMEM((HERE, MODEL_DIM), BF16),
            pltpu.VMEM((HERE, MODEL_DIM), BF16),
            pltpu.VMEM((6, MODEL_DIM, SHARD), BF16),
            pltpu.VMEM((768, MODEL_DIM), BF16),
            pltpu.VMEM((MODEL_DIM, 2 * MODEL_DIM), BF16),
            pltpu.VMEM((MODEL_DIM, MODEL_DIM), BF16),
            pltpu.VMEM((LONG, 2, HALF, BLOCK), F32),
            pltpu.VMEM((HERE, MODEL_DIM), BF16),
            pltpu.VMEM((8, HEAD_DIM, HERE), BF16),
            pltpu.VMEM((8, 2, HEAD_DIM, HERE), BF16),
            pltpu.VMEM((8, BLOCK, HERE), BF16),
            pltpu.VMEM((8, 2, BLOCK, 2 * HERE), BF16),
            pltpu.VMEM((2 * HERE, BLOCK), BF16),
            pltpu.VMEM((8, 1, HERE), F32),
            pltpu.VMEM((8, 112, HERE), F32),
            pltpu.VMEM((8, HEAD_DIM, HERE), BF16),
            pltpu.VMEM((8, HEAD_DIM, HERE), BF16),
            pltpu.VMEM((HERE, MODEL_DIM), F32),
            pltpu.VMEM((HERE, MODEL_DIM), F32),
            pltpu.VMEM((HERE + 32, MODEL_DIM), BF16),
            pltpu.VMEM((2, 160, BLOCK), F32),
            dma((16,)), dma((6,)), dma((8,)), dma((8,)), dma((8,)), dma((8,)), dma((8,)), dma((8,)), dma((8,)), dma((8,)),
            dma((2, 9)), dma((2, 9)), dma((2, 7)), dma((2, 7)), dma((2, 4)), dma((2, 4)),
        ],
        compiler_params=pltpu.CompilerParams(
            collective_id=0, has_side_effects=True, vmem_limit_bytes=56 * 1024 * 1024
        ),
        name="conformer",
    )(
        inputs, block_ids, attn_gain, w_qkv, w_out, conv_gain, conv_in, depthwise_w,
        depth_gain, conv_out, jnp.asarray(rotation_tables()),
    )


def solution(mesh):
    return jax.shard_map(
        local,
        mesh=mesh,
        in_specs=(
            P("dp", "ctx", None),
            P("dp", None),
            P(),
            P(),
            P(),
            P(),
            P(None, "dp"),
            P(),
            P(),
            P(),
        ),
        out_specs=P("dp", "ctx", None),
        check_vma=False,
    )
```

```python
import functools
import math

import jax
import jax.numpy as jnp
import numpy as np
from jax import lax
from jax.experimental import pallas as pl
from jax.experimental.pallas import tpu as pltpu
from jax.sharding import PartitionSpec as P

MODEL_DIM = 1536
HEAD_COUNT = 8
HEAD_DIM = 96
HALF = HEAD_DIM // 2
KERNEL = 31
BLOCK = 128
BLOCKS = 32
LONG = 24
AWAY = -1e30
HERE = 256
SHARD = 384
EPSILON = 1e-05
MESH = pl.DeviceIdType.MESH
F32 = jnp.float32
BF16 = jnp.bfloat16


def rotation_tables():
    inverse = 10000.0 ** (-np.arange(HALF, dtype=np.float64) / HALF)
    angles = np.arange(LONG * BLOCK, dtype=np.float64)[None, :] * inverse[:, None]
    pair = np.stack([np.cos(angles), np.sin(angles)])
    pair = pair.reshape(2, HALF, LONG, BLOCK).transpose(2, 0, 1, 3)
    return np.ascontiguousarray(pair).astype(np.float32)


def norm(values, gain):
    average = jnp.mean(values, axis=-1, keepdims=True)
    centred = values - average
    variance = jnp.mean(centred * centred, axis=-1, keepdims=True)
    return centred * lax.rsqrt(variance + EPSILON) * gain


def flip(index, off):
    out = index
    for bit in (1, 2, 4):
        out = out + bit * ((off // bit) % 2) * (1 - 2 * ((index // bit) % 2))
    return out


def kernel(
    x_hbm, ids_hbm, attn_hbm, wqkv_hbm, wout_hbm, conv_hbm, cin_hbm, dw_hbm, depth_hbm, cout_hbm, tab_hbm,
    out_hbm,
    ids, attn_gain, conv_gain, depth_gain, dw, out, xv, wq, wo, cw, co, tab, normed, sq, skv, qbuf, kvbuf, kn, peaks, totals, osend, att, resid, filt, ext, tmp,
    load_sem, wq_sem, q_send, q_recv, kv_send, kv_recv, fwd_send, fwd_recv, o_send, o_recv,
    g_send, g_recv, s_send, s_recv, h_send, h_recv,
):
    d = lax.axis_index("dp")
    c = lax.axis_index("ctx")
    chip, core = c // 2, c % 2
    sibling = (d, c + 1 - 2 * core)
    z, yh = d // 2, d % 2
    zp, zm, z2 = (z + 1) % 4, (z + 3) % 4, (z + 2) % 4
    other = 1 - yh
    across = (2 * z + other, c + 2 - 4 * (chip % 2))
    up, down = (2 * zp + yh, c), (2 * zm + yh, c)
    right, left = (d, (c + 1) % 16), (d, (c + 15) % 16)

    def peer(off):
        return (d, 2 * flip(chip, off) + core)

    barrier = pltpu.get_barrier_semaphore()
    cross = (d, lax.select(core == 0, (c + 15) % 16, (c + 1) % 16))
    greeted = [peer(off) for off in range(1, 8)] + [sibling, across, up, down, cross]
    for device in greeted:
        pl.semaphore_signal(barrier, inc=1, device_id=device, device_id_type=MESH)

    def shard_cols(dd):
        return pl.ds(pl.multiple_of(SHARD * (2 * (dd % 4) + dd // 4), 128), SHARD)

    loads = [
        pltpu.make_async_copy(x_hbm.at[0], xv, load_sem.at[0]),
        pltpu.make_async_copy(tab_hbm, tab, load_sem.at[1]),
        pltpu.make_async_copy(wout_hbm, wo, load_sem.at[2]),
        pltpu.make_async_copy(cout_hbm, co, load_sem.at[3]),
        pltpu.make_async_copy(cin_hbm, cw.at[:, shard_cols(d)], load_sem.at[4]),
    ]
    small = [
        pltpu.make_async_copy(src, dst, load_sem.at[8 + n])
        for n, (src, dst) in enumerate(
            ((attn_hbm, attn_gain), (ids_hbm, ids), (conv_hbm, conv_gain), (depth_hbm, depth_gain), (dw_hbm, dw))
        )
    ]
    loads[0].start()
    small[0].start()
    small[1].start()
    far, near = 1 - chip // 4, chip // 4
    steps = ((0, far), (0, near), (1, far), (2, far), (1, near), (2, near))
    wq_copies = []
    for slot, (kind, group) in enumerate(steps):
        start = pl.multiple_of(768 * kind + SHARD * group, 128)
        copy = pltpu.make_async_copy(wqkv_hbm.at[:, pl.ds(start, SHARD)], wq.at[slot], wq_sem.at[slot])
        copy.start()
        wq_copies.append(copy)
        if slot == 0:
            loads[1].start()
    for copy in small[2:] + loads[2:]:
        copy.start()

    def remote(src, dst, device, ssem, rsem):
        return pltpu.make_async_remote_copy(
            src_ref=src, dst_ref=dst, send_sem=ssem, recv_sem=rsem, device_id=device, device_id_type=MESH
        )

    loads[0].wait()
    small[0].wait()

    def norm_rows(i, _):
        rows = pl.ds(pl.multiple_of(256 * i, 256), 256)
        normed[rows, :] = norm(xv[rows, :].astype(F32), attn_gain[...]).astype(BF16)
        return _

    lax.fori_loop(0, HERE // 256, norm_rows, 0)

    a_up, a_down, a_far = 2 * zp + yh, 2 * zm + yh, 2 * z2 + yh
    b_here, b_up, b_down, b_far = 2 * z + other, 2 * zp + other, 2 * zm + other, 2 * z2 + other

    def piece(dd, p, of=core):
        return cw.at[pl.ds(pl.multiple_of(768 * of + 384 * p, 384), 384), shard_cols(dd)]

    def third(dd, p, n):
        rows = pl.ds(pl.multiple_of(768 * core + 384 * p + 128 * n, 128), 128)
        return cw.at[rows, shard_cols(dd)]

    def gather(src, dst, device, p, n):
        return remote(src, dst, device, g_send.at[p, n], g_recv.at[p, n])

    def start_all(copies):
        for copy in copies:
            copy.start()

    def gather_wait(ref, p, n):
        remote(ref, ref, up, g_send.at[p, n], g_recv.at[p, n]).wait_recv()

    def to_sibling(dd, p, n):
        return remote(piece(dd, p), piece(dd, p), sibling, s_send.at[p, n], s_recv.at[p, n])

    def from_sibling(dd, n):
        for p in range(2):
            ref = piece(dd, p, 1 - core)
            remote(ref, ref, sibling, s_send.at[p, n], s_recv.at[p, n]).wait_recv()

    def gather_1(p):
        own = cin_hbm.at[pl.ds(pl.multiple_of(768 * core + 384 * p, 384), 384)]
        return [
            gather(own, piece(d, p), down, p, 0),
            gather(own, piece(d, p), across, p, 1),
            gather(own, piece(d, p), up, p, 2),
        ]

    def gather_2(p):
        return [
            gather(piece(a_up, p), piece(a_up, p), down, p, 3),
            gather(piece(a_up, p), piece(a_up, p), across, p, 4),
            gather(piece(b_here, p), piece(b_here, p), up, p, 5),
            to_sibling(a_up, p, 0),
            to_sibling(b_here, p, 1),
            to_sibling(a_down, p, 2),
        ]

    def gather_3(p):
        return [
            gather(third(a_far, p, 0), third(a_far, p, 0), across, p, 6),
            gather(third(b_up, p, 1), third(b_up, p, 1), down, p, 7),
            gather(third(b_down, p, 2), third(b_down, p, 2), up, p, 8),
            to_sibling(a_far, p, 3),
            to_sibling(b_up, p, 4),
            to_sibling(b_down, p, 5),
        ]

    def gather_4(p):
        return [to_sibling(b_far, p, 6)]

    def run_2(p):
        gather_wait(piece(a_up, p), p, 0)
        gather_wait(piece(b_here, p), p, 1)
        gather_wait(piece(a_down, p), p, 2)
        start_all(gather_2(p))

    def run_3(p):
        gather_wait(piece(a_far, p), p, 3)
        gather_wait(piece(b_up, p), p, 4)
        gather_wait(piece(b_down, p), p, 5)
        start_all(gather_3(p))

    def run_4(p):
        for n in range(3):
            gather_wait(third(b_far, p, n), p, 6 + n)
        start_all(gather_4(p))

    small[1].wait()
    place = []
    for t in range(2):
        mine = ids[0, 2 * c + t]
        earlier = jnp.int32(0)
        for j in range(BLOCKS):
            earlier = earlier + (ids[0, j] < mine).astype(jnp.int32)
        place.append(lax.min(2 * c + t - earlier, LONG - 1))
    loads[1].wait()
    cosine = jnp.concatenate([tab[place[0], 0], tab[place[1], 0]], axis=1)
    sine = jnp.concatenate([tab[place[0], 1], tab[place[1], 1]], axis=1)
    scale = math.log2(math.e) / math.sqrt(HEAD_DIM)

    def q_slot(i):
        return qbuf.at[i, pl.ds(0, HEAD_DIM)]

    def kv_slot(i, of):
        return kvbuf.at[i, :, pl.ds(0, HEAD_DIM), pl.ds(pl.multiple_of(HERE * of, HERE), HERE)]

    sends = []
    for slot, (kind, group) in enumerate(steps):
        wq_copies[slot].wait()
        turned = jnp.transpose(jnp.dot(normed[...], wq[slot], preferred_element_type=F32))
        for i in range(4):
            first = turned[96 * i : 96 * i + 48]
            second = turned[96 * i + 48 : 96 * i + 96]
            if kind < 2:
                first, second = first * cosine - second * sine, second * cosine + first * sine
            if kind == 0:
                sq[4 * group + i, 0:48, :] = (first * scale).astype(BF16)
                sq[4 * group + i, 48:96, :] = (second * scale).astype(BF16)
            else:
                skv[4 * group + i, kind - 1, 0:48, :] = first.astype(BF16)
                skv[4 * group + i, kind - 1, 48:96, :] = second.astype(BF16)
        if slot == 1:
            pl.semaphore_wait(barrier, len(greeted))
            for off in range(1, 8):
                to = flip(chip, off)
                sends.append(remote(sq.at[to], q_slot(chip), peer(off), q_send.at[off], q_recv.at[off]))
                sends[-1].start()
            start_all(gather_1(0))
            start_all(gather_1(1))
        if slot in (3, 5):
            for off in (range(4, 8) if slot == 3 else range(1, 4)):
                to = flip(chip, off)
                sends.append(remote(skv.at[to], kv_slot(chip, core), peer(off), kv_send.at[off], kv_recv.at[off]))
                sends[-1].start()
    keep_q = pltpu.make_async_copy(sq.at[chip], q_slot(chip), load_sem.at[5])
    keep_kv = pltpu.make_async_copy(skv.at[chip], kv_slot(chip, core), load_sem.at[6])
    keep_q.start()
    keep_kv.start()

    def forward(off, src):
        return remote(src, kv_slot(flip(chip, off), core), sibling, fwd_send.at[off], fwd_recv.at[off])

    forward(0, skv.at[chip]).start()

    row = lax.broadcasted_iota(jnp.int32, (BLOCK - HEAD_DIM, BLOCK), 0)

    def mark_keys(j, _):
        spot = pl.ds(pl.multiple_of(BLOCK * (j % 4), BLOCK), BLOCK)
        kvbuf[j // 4, 0, HEAD_DIM:, spot] = jnp.where(row == ids[0, j], 1.0, 0.0).astype(BF16)
        kvbuf[j // 4, 1, HEAD_DIM:, spot] = jnp.ones((BLOCK - HEAD_DIM, BLOCK), BF16)
        return _

    def mark_queries(j, _):
        spot = pl.ds(pl.multiple_of(BLOCK * (j % 2), BLOCK), BLOCK)
        mine = ids[0, 4 * (j // 2) + 2 * core + j % 2]
        qbuf[j // 2, HEAD_DIM:, spot] = jnp.where(row == mine, 0.0, AWAY).astype(BF16)
        return _

    lax.fori_loop(0, BLOCKS, mark_keys, 0)
    lax.fori_loop(0, 16, mark_queries, 0)
    peaks[...] = jnp.full(peaks.shape, -3e38, F32)
    totals[...] = jnp.zeros(totals.shape, F32)

    keep_q.wait()
    for off in range(1, 8):
        slot = q_slot(flip(chip, off))
        remote(slot, slot, peer(off), q_send.at[off], q_recv.at[off]).wait_recv()
    keep_kv.wait()

    def order(n):
        return lax.select(n < 5, n + 3, n - 4)

    def arrive(off):
        slot = kv_slot(flip(chip, off), core)
        remote(slot, slot, peer(off), kv_send.at[off], kv_recv.at[off]).wait_recv()
        forward(off, slot).start()

    def keys_of(off):
        source = flip(chip, off)
        slot = kv_slot(source, 1 - core)
        remote(slot, slot, sibling, fwd_send.at[off], fwd_recv.at[off]).wait_recv()
        kn[...] = jnp.transpose(kvbuf[source, 0])
        return source

    def attend(source, tiles, last=False):
        scores = [jnp.dot(kn[...], qbuf[i], preferred_element_type=F32) for i in tiles]
        results = []
        for i, score in zip(tiles, scores):
            old = peaks[i]
            top = jnp.maximum(old, jnp.max(score, axis=0, keepdims=True))
            if not last:
                peaks[i] = top
            weights = jnp.exp2(score - top).astype(BF16)
            fresh = jnp.dot(kvbuf[source, 1, 0:112, :], weights, preferred_element_type=F32)
            results.append(totals[i] * jnp.exp2(old - top) + fresh)
        return results

    def use_source(n, _):
        arrive(order(n + 1))
        pl.when(n == 2)(lambda: run_2(0))
        pl.when(n == 5)(lambda: run_2(1))
        source = keys_of(lax.select(n == 0, 0, order(n)))
        for i, total in enumerate(attend(source, range(8))):
            totals[i] = total
        return _

    lax.fori_loop(0, 7, use_source, 0)
    source = keys_of(order(7))

    def o_copy(i, off):
        return remote(osend.at[i], att.at[chip], (d, 2 * i + core), o_send.at[off], o_recv.at[off])

    for offs in ((6, 7, 4, 5), (2, 3, 1, 0)):
        tiles = [flip(chip, off) for off in offs]
        for off, i, total in zip(offs, tiles, attend(source, tiles, last=True)):
            osend[i] = (total[0:96] / total[96:97]).astype(BF16)
            if off:
                o_copy(i, off).start()
    o_keep = pltpu.make_async_copy(osend.at[chip], att.at[chip], load_sem.at[7])
    o_keep.start()

    run_3(0)
    loads[2].wait()
    o_keep.wait()
    for off in range(1, 8):
        slot = att.at[flip(chip, off)]
        remote(slot, slot, peer(off), o_send.at[off], o_recv.at[off]).wait_recv()
    normed[:, 0:768] = jnp.transpose(att[...].reshape(768, HERE))

    def add_out(i):
        cols = slice(512 * i, 512 * i + 512)
        resid[:, cols] = xv[:, cols].astype(F32) + jnp.dot(
            normed[:, 0:768], wo[:, cols], preferred_element_type=F32
        )

    for i in range(3):
        add_out(i)
    run_3(1)

    small[2].wait()

    def norm_residual(i, _):
        rows = pl.ds(pl.multiple_of(256 * i, 256), 256)
        normed[rows, :] = norm(resid[rows, :], conv_gain[...]).astype(BF16)
        return _

    lax.fori_loop(0, HERE // 256, norm_residual, 0)

    def edge_copies(n, v):
        cols = pl.ds(pl.multiple_of(SHARD * v, 128), SHARD)
        return [
            remote(ext.at[pl.ds(256, 16), cols], ext.at[pl.ds(0, 16), cols], right, h_send.at[0, n], h_recv.at[0, n]),
            remote(ext.at[pl.ds(16, 16), cols], ext.at[pl.ds(272, 16), cols], left, h_send.at[1, n], h_recv.at[1, n]),
        ]

    edges = []

    def gate(n, v):
        cols = pl.ds(pl.multiple_of(SHARD * v, 128), SHARD)
        both = pl.ds(pl.multiple_of(2 * SHARD * v, 256), 2 * SHARD)
        wide = jnp.dot(normed[...], cw[:, both], preferred_element_type=F32)
        ext[16:272, cols] = (wide[:, :SHARD] * jax.nn.sigmoid(wide[:, SHARD:])).astype(BF16)
        for copy in edge_copies(n, v):
            copy.start()
            edges.append(copy)

    here_0, here_1 = ids[0, 2 * c], ids[0, 2 * c + 1]
    before = ids[0, lax.max(2 * c - 1, 0)]
    after = ids[0, lax.min(2 * c + 2, BLOCKS - 1)]
    inner = here_0 == here_1
    keeps = (
        (jnp.logical_and(c > 0, before == here_0), inner),
        (inner, jnp.logical_and(c < 15, after == here_1)),
    )

    def taps(n, v):
        for copy in edge_copies(n, v):
            copy.wait_recv()

        def filter_lanes(i, _):
            cols = pl.ds(pl.multiple_of(SHARD * v + BLOCK * i, BLOCK), BLOCK)
            for t in range(2):
                head = ext[BLOCK * t : BLOCK * t + 16, cols].astype(F32)
                tail = ext[BLOCK * t + 144 : BLOCK * t + 160, cols].astype(F32)
                tmp[t, 0:16, :] = jnp.where(keeps[t][0], head, 0.0)
                tmp[t, 16:144, :] = ext[BLOCK * t + 16 : BLOCK * t + 144, cols].astype(F32)
                tmp[t, 144:160, :] = jnp.where(keeps[t][1], tail, 0.0)
                total = jnp.zeros((BLOCK, BLOCK), F32)
                for tap in range(KERNEL):
                    total += dw[tap : tap + 1, cols] * tmp[t, tap + 1 : tap + 1 + BLOCK, :]
                filt[BLOCK * t : BLOCK * t + BLOCK, cols] = total
            return _

        lax.fori_loop(0, 3, filter_lanes, 0)

    groups = (a_up % 4, b_up % 4, d % 4, b_here % 4)
    for n in (0, 2):
        from_sibling((a_up, 0, a_down)[n], n)
    gate(0, groups[0])
    small[3].wait()
    small[4].wait()
    for n, dd in ((4, b_up), (5, b_down)):
        from_sibling(dd, n)
    gate(1, groups[1])
    run_4(0)
    loads[4].wait()
    from_sibling(a_far, 3)
    gate(2, groups[2])
    run_4(1)
    taps(0, groups[0])
    for n, dd in ((1, b_here), (6, b_far)):
        from_sibling(dd, n)
    gate(3, groups[3])
    for n in range(1, 4):
        taps(n, groups[n])

    def norm_filtered(i, _):
        rows = pl.ds(pl.multiple_of(256 * i, 256), 256)
        values = norm(filt[rows, :], depth_gain[...])
        normed[rows, :] = (values / (1.0 + jnp.exp(-values))).astype(BF16)
        return _

    lax.fori_loop(0, HERE // 256, norm_filtered, 0)

    loads[3].wait()

    def out_copy(i):
        cols = pl.ds(512 * i, 512)
        return pltpu.make_async_copy(out.at[:, cols], out_hbm.at[0, :, cols], load_sem.at[13 + i])

    def add_conv(i):
        cols = slice(512 * i, 512 * i + 512)
        out[:, cols] = (
            resid[:, cols] + jnp.dot(normed[...], co[:, cols], preferred_element_type=F32)
        ).astype(BF16)
        out_copy(i).start()

    for i in range(3):
        add_conv(i)

    gathers = [copy for p in range(2) for step in (gather_1, gather_2, gather_3, gather_4) for copy in step(p)]
    for copy in gathers + sends + edges:
        copy.wait_send()
    forward(0, skv.at[chip]).wait_send()

    def drain(off, _):
        forward(off, kv_slot(flip(chip, off), core)).wait_send()
        o_copy(flip(chip, off), off).wait_send()
        return _

    lax.fori_loop(1, 8, drain, 0)
    for i in range(3):
        out_copy(i).wait()


def local(inputs, block_ids, attn_gain, w_qkv, w_out, conv_gain, conv_in, depthwise_w, depth_gain, conv_out):
    in_hbm = pl.BlockSpec(memory_space=pl.ANY)
    dma = pltpu.SemaphoreType.DMA
    return pl.pallas_call(
        kernel,
        out_shape=jax.ShapeDtypeStruct((1, HERE, MODEL_DIM), BF16),
        in_specs=[in_hbm] * 11,
        out_specs=in_hbm,
        scratch_shapes=[
            pltpu.SMEM((1, BLOCKS), jnp.int32),
            pltpu.VMEM((MODEL_DIM,), F32),
            pltpu.VMEM((MODEL_DIM,), F32),
            pltpu.VMEM((MODEL_DIM,), F32),
            pltpu.VMEM((KERNEL, MODEL_DIM), F32),
            pltpu.VMEM((HERE, MODEL_DIM), BF16),
            pltpu.VMEM((HERE, MODEL_DIM), BF16),
            pltpu.VMEM((6, MODEL_DIM, SHARD), BF16),
            pltpu.VMEM((768, MODEL_DIM), BF16),
            pltpu.VMEM((MODEL_DIM, 2 * MODEL_DIM), BF16),
            pltpu.VMEM((MODEL_DIM, MODEL_DIM), BF16),
            pltpu.VMEM((LONG, 2, HALF, BLOCK), F32),
            pltpu.VMEM((HERE, MODEL_DIM), BF16),
            pltpu.VMEM((8, HEAD_DIM, HERE), BF16),
            pltpu.VMEM((8, 2, HEAD_DIM, HERE), BF16),
            pltpu.VMEM((8, BLOCK, HERE), BF16),
            pltpu.VMEM((8, 2, BLOCK, 2 * HERE), BF16),
            pltpu.VMEM((2 * HERE, BLOCK), BF16),
            pltpu.VMEM((8, 1, HERE), F32),
            pltpu.VMEM((8, 112, HERE), F32),
            pltpu.VMEM((8, HEAD_DIM, HERE), BF16),
            pltpu.VMEM((8, HEAD_DIM, HERE), BF16),
            pltpu.VMEM((HERE, MODEL_DIM), F32),
            pltpu.VMEM((HERE, MODEL_DIM), F32),
            pltpu.VMEM((HERE + 32, MODEL_DIM), BF16),
            pltpu.VMEM((2, 160, BLOCK), F32),
            dma((16,)), dma((6,)), dma((8,)), dma((8,)), dma((8,)), dma((8,)), dma((8,)), dma((8,)), dma((8,)), dma((8,)),
            dma((2, 9)), dma((2, 9)), dma((2, 7)), dma((2, 7)), dma((2, 4)), dma((2, 4)),
        ],
        compiler_params=pltpu.CompilerParams(
            collective_id=0, has_side_effects=True, vmem_limit_bytes=56 * 1024 * 1024
        ),
        name="conformer",
    )(
        inputs, block_ids, attn_gain, w_qkv, w_out, conv_gain, conv_in, depthwise_w,
        depth_gain, conv_out, jnp.asarray(rotation_tables()),
    )


def solution(mesh):
    return jax.shard_map(
        local,
        mesh=mesh,
        in_specs=(
            P("dp", "ctx", None),
            P("dp", None),
            P(),
            P(),
            P(),
            P(),
            P(None, "dp"),
            P(),
            P(),
            P(),
        ),
        out_specs=P("dp", "ctx", None),
        check_vma=False,
    )
```

```python
import functools
import math

import jax
import jax.numpy as jnp
import numpy as np
from jax import lax
from jax.experimental import pallas as pl
from jax.experimental.pallas import tpu as pltpu
from jax.sharding import PartitionSpec as P

MODEL_DIM = 1536
HEAD_COUNT = 8
HEAD_DIM = 96
HALF = HEAD_DIM // 2
KERNEL = 31
BLOCK = 128
BLOCKS = 32
LONG = 24
AWAY = -1e30
HERE = 256
SHARD = 384
EPSILON = 1e-05
MESH = pl.DeviceIdType.MESH
F32 = jnp.float32
BF16 = jnp.bfloat16


def rotation_tables():
    inverse = 10000.0 ** (-np.arange(HALF, dtype=np.float64) / HALF)
    angles = np.arange(LONG * BLOCK, dtype=np.float64)[None, :] * inverse[:, None]
    pair = np.stack([np.cos(angles), np.sin(angles)])
    pair = pair.reshape(2, HALF, LONG, BLOCK).transpose(2, 0, 1, 3)
    return np.ascontiguousarray(pair).astype(np.float32)


def norm(values, gain):
    average = jnp.mean(values, axis=-1, keepdims=True)
    centred = values - average
    variance = jnp.mean(centred * centred, axis=-1, keepdims=True)
    return centred * lax.rsqrt(variance + EPSILON) * gain


def flip(index, off):
    out = index
    for bit in (1, 2, 4):
        out = out + bit * ((off // bit) % 2) * (1 - 2 * ((index // bit) % 2))
    return out


def kernel(
    x_hbm, ids_hbm, attn_hbm, wqkv_hbm, wout_hbm, conv_hbm, cin_hbm, dw_hbm, depth_hbm, cout_hbm, tab_hbm,
    out_hbm,
    ids, attn_gain, conv_gain, depth_gain, dw, out, xv, wq, wo, cw, co, tab, normed, sq, skv, qbuf, kvbuf, kn, peaks, totals, osend, att, resid, filt, ext, tmp,
    load_sem, wq_sem, q_send, q_recv, kv_send, kv_recv, fwd_send, fwd_recv, o_send, o_recv,
    g_send, g_recv, s_send, s_recv, h_send, h_recv,
):
    d = lax.axis_index("dp")
    c = lax.axis_index("ctx")
    chip, core = c // 2, c % 2
    sibling = (d, c + 1 - 2 * core)
    z, yh = d // 2, d % 2
    zp, zm, z2 = (z + 1) % 4, (z + 3) % 4, (z + 2) % 4
    other = 1 - yh
    across = (2 * z + other, c + 2 - 4 * (chip % 2))
    up, down = (2 * zp + yh, c), (2 * zm + yh, c)
    right, left = (d, (c + 1) % 16), (d, (c + 15) % 16)

    def peer(off):
        return (d, 2 * flip(chip, off) + core)

    barrier = pltpu.get_barrier_semaphore()
    cross = (d, lax.select(core == 0, (c + 15) % 16, (c + 1) % 16))
    greeted = [peer(off) for off in range(1, 8)] + [sibling, across, up, down, cross]
    for device in greeted:
        pl.semaphore_signal(barrier, inc=1, device_id=device, device_id_type=MESH)

    def shard_cols(dd):
        return pl.ds(pl.multiple_of(SHARD * (2 * (dd % 4) + dd // 4), 128), SHARD)

    loads = [
        pltpu.make_async_copy(x_hbm.at[0], xv, load_sem.at[0]),
        pltpu.make_async_copy(tab_hbm, tab, load_sem.at[1]),
        pltpu.make_async_copy(wout_hbm, wo, load_sem.at[2]),
        pltpu.make_async_copy(cout_hbm, co, load_sem.at[3]),
        pltpu.make_async_copy(cin_hbm, cw.at[:, shard_cols(d)], load_sem.at[4]),
    ]
    small = [
        pltpu.make_async_copy(src, dst, load_sem.at[8 + n])
        for n, (src, dst) in enumerate(
            ((attn_hbm, attn_gain), (ids_hbm, ids), (conv_hbm, conv_gain), (depth_hbm, depth_gain), (dw_hbm, dw))
        )
    ]
    loads[0].start()
    small[0].start()
    small[1].start()
    far, near = 1 - chip // 4, chip // 4
    steps = ((0, far), (0, near), (1, far), (2, far), (1, near), (2, near))
    wq_copies = []
    for slot, (kind, group) in enumerate(steps):
        start = pl.multiple_of(768 * kind + SHARD * group, 128)
        copy = pltpu.make_async_copy(wqkv_hbm.at[:, pl.ds(start, SHARD)], wq.at[slot], wq_sem.at[slot])
        copy.start()
        wq_copies.append(copy)
        if slot == 0:
            loads[1].start()
    for copy in small[2:] + loads[2:]:
        copy.start()

    def remote(src, dst, device, ssem, rsem):
        return pltpu.make_async_remote_copy(
            src_ref=src, dst_ref=dst, send_sem=ssem, recv_sem=rsem, device_id=device, device_id_type=MESH
        )

    loads[0].wait()
    small[0].wait()

    def norm_rows(i, _):
        rows = pl.ds(pl.multiple_of(256 * i, 256), 256)
        normed[rows, :] = norm(xv[rows, :].astype(F32), attn_gain[...]).astype(BF16)
        return _

    lax.fori_loop(0, HERE // 256, norm_rows, 0)

    a_up, a_down, a_far = 2 * zp + yh, 2 * zm + yh, 2 * z2 + yh
    b_here, b_up, b_down, b_far = 2 * z + other, 2 * zp + other, 2 * zm + other, 2 * z2 + other

    def piece(dd, p, of=core):
        return cw.at[pl.ds(pl.multiple_of(768 * of + 384 * p, 384), 384), shard_cols(dd)]

    def third(dd, p, n):
        rows = pl.ds(pl.multiple_of(768 * core + 384 * p + 128 * n, 128), 128)
        return cw.at[rows, shard_cols(dd)]

    def gather(src, dst, device, p, n):
        return remote(src, dst, device, g_send.at[p, n], g_recv.at[p, n])

    def start_all(copies):
        for copy in copies:
            copy.start()

    def gather_wait(ref, p, n):
        remote(ref, ref, up, g_send.at[p, n], g_recv.at[p, n]).wait_recv()

    def to_sibling(dd, p, n):
        return remote(piece(dd, p), piece(dd, p), sibling, s_send.at[p, n], s_recv.at[p, n])

    def from_sibling(dd, n):
        for p in range(2):
            ref = piece(dd, p, 1 - core)
            remote(ref, ref, sibling, s_send.at[p, n], s_recv.at[p, n]).wait_recv()

    def gather_1(p):
        own = cin_hbm.at[pl.ds(pl.multiple_of(768 * core + 384 * p, 384), 384)]
        return [
            gather(own, piece(d, p), down, p, 0),
            gather(own, piece(d, p), across, p, 1),
            gather(own, piece(d, p), up, p, 2),
        ]

    def gather_2(p):
        return [
            gather(piece(a_up, p), piece(a_up, p), down, p, 3),
            gather(piece(a_up, p), piece(a_up, p), across, p, 4),
            gather(piece(b_here, p), piece(b_here, p), up, p, 5),
            to_sibling(a_up, p, 0),
            to_sibling(b_here, p, 1),
            to_sibling(a_down, p, 2),
        ]

    def gather_3(p):
        return [
            gather(third(a_far, p, 0), third(a_far, p, 0), across, p, 6),
            gather(third(b_up, p, 1), third(b_up, p, 1), down, p, 7),
            gather(third(b_down, p, 2), third(b_down, p, 2), up, p, 8),
            to_sibling(a_far, p, 3),
            to_sibling(b_up, p, 4),
            to_sibling(b_down, p, 5),
        ]

    def gather_4(p):
        return [to_sibling(b_far, p, 6)]

    def run_2(p):
        gather_wait(piece(a_up, p), p, 0)
        gather_wait(piece(b_here, p), p, 1)
        gather_wait(piece(a_down, p), p, 2)
        start_all(gather_2(p))

    def run_3(p):
        gather_wait(piece(a_far, p), p, 3)
        gather_wait(piece(b_up, p), p, 4)
        gather_wait(piece(b_down, p), p, 5)
        start_all(gather_3(p))

    def run_4(p):
        for n in range(3):
            gather_wait(third(b_far, p, n), p, 6 + n)
        start_all(gather_4(p))

    small[1].wait()
    place = []
    for t in range(2):
        mine = ids[0, 2 * c + t]
        earlier = jnp.int32(0)
        for j in range(BLOCKS):
            earlier = earlier + (ids[0, j] < mine).astype(jnp.int32)
        place.append(lax.min(2 * c + t - earlier, LONG - 1))
    loads[1].wait()
    cosine = jnp.concatenate([tab[place[0], 0], tab[place[1], 0]], axis=1)
    sine = jnp.concatenate([tab[place[0], 1], tab[place[1], 1]], axis=1)
    scale = math.log2(math.e) / math.sqrt(HEAD_DIM)

    def q_slot(i):
        return qbuf.at[i, pl.ds(0, HEAD_DIM)]

    def kv_slot(i, of):
        return kvbuf.at[i, :, pl.ds(0, HEAD_DIM), pl.ds(pl.multiple_of(HERE * of, HERE), HERE)]

    sends = []
    for slot, (kind, group) in enumerate(steps):
        wq_copies[slot].wait()
        turned = jnp.transpose(jnp.dot(normed[...], wq[slot], preferred_element_type=F32))
        for i in range(4):
            first = turned[96 * i : 96 * i + 48]
            second = turned[96 * i + 48 : 96 * i + 96]
            if kind < 2:
                first, second = first * cosine - second * sine, second * cosine + first * sine
            if kind == 0:
                sq[4 * group + i, 0:48, :] = (first * scale).astype(BF16)
                sq[4 * group + i, 48:96, :] = (second * scale).astype(BF16)
            else:
                skv[4 * group + i, kind - 1, 0:48, :] = first.astype(BF16)
                skv[4 * group + i, kind - 1, 48:96, :] = second.astype(BF16)
        if slot == 1:
            pl.semaphore_wait(barrier, len(greeted))
            for off in range(1, 8):
                to = flip(chip, off)
                sends.append(remote(sq.at[to], q_slot(chip), peer(off), q_send.at[off], q_recv.at[off]))
                sends[-1].start()
            start_all(gather_1(0))
            start_all(gather_1(1))
        if slot in (3, 5):
            for off in (range(4, 8) if slot == 3 else range(1, 4)):
                to = flip(chip, off)
                sends.append(remote(skv.at[to], kv_slot(chip, core), peer(off), kv_send.at[off], kv_recv.at[off]))
                sends[-1].start()
    keep_q = pltpu.make_async_copy(sq.at[chip], q_slot(chip), load_sem.at[5])
    keep_kv = pltpu.make_async_copy(skv.at[chip], kv_slot(chip, core), load_sem.at[6])
    keep_q.start()
    keep_kv.start()

    def forward(off, src):
        return remote(src, kv_slot(flip(chip, off), core), sibling, fwd_send.at[off], fwd_recv.at[off])

    forward(0, skv.at[chip]).start()

    row = lax.broadcasted_iota(jnp.int32, (BLOCK - HEAD_DIM, BLOCK), 0)

    def mark_keys(j, _):
        spot = pl.ds(pl.multiple_of(BLOCK * (j % 4), BLOCK), BLOCK)
        kvbuf[j // 4, 0, HEAD_DIM:, spot] = jnp.where(row == ids[0, j], 1.0, 0.0).astype(BF16)
        kvbuf[j // 4, 1, HEAD_DIM:, spot] = jnp.ones((BLOCK - HEAD_DIM, BLOCK), BF16)
        return _

    def mark_queries(j, _):
        spot = pl.ds(pl.multiple_of(BLOCK * (j % 2), BLOCK), BLOCK)
        mine = ids[0, 4 * (j // 2) + 2 * core + j % 2]
        qbuf[j // 2, HEAD_DIM:, spot] = jnp.where(row == mine, 0.0, AWAY).astype(BF16)
        return _

    lax.fori_loop(0, BLOCKS, mark_keys, 0)
    lax.fori_loop(0, 16, mark_queries, 0)
    peaks[...] = jnp.full(peaks.shape, -3e38, F32)
    totals[...] = jnp.zeros(totals.shape, F32)

    keep_q.wait()
    for off in range(1, 8):
        slot = q_slot(flip(chip, off))
        remote(slot, slot, peer(off), q_send.at[off], q_recv.at[off]).wait_recv()
    keep_kv.wait()

    def order(n):
        return lax.select(n < 5, n + 3, n - 4)

    def arrive(off):
        slot = kv_slot(flip(chip, off), core)
        remote(slot, slot, peer(off), kv_send.at[off], kv_recv.at[off]).wait_recv()
        forward(off, slot).start()

    def keys_of(off):
        source = flip(chip, off)
        slot = kv_slot(source, 1 - core)
        remote(slot, slot, sibling, fwd_send.at[off], fwd_recv.at[off]).wait_recv()
        kn[...] = jnp.transpose(kvbuf[source, 0])
        return source

    def attend(source, tiles, last=False):
        scores = [jnp.dot(kn[...], qbuf[i], preferred_element_type=F32) for i in tiles]
        results = []
        for i, score in zip(tiles, scores):
            old = peaks[i]
            top = jnp.maximum(old, jnp.max(score, axis=0, keepdims=True))
            if not last:
                peaks[i] = top
            weights = jnp.exp2(score - top).astype(BF16)
            fresh = jnp.dot(kvbuf[source, 1, 0:112, :], weights, preferred_element_type=F32)
            results.append(totals[i] * jnp.exp2(old - top) + fresh)
        return results

    def use_source(n, _):
        arrive(order(n + 1))
        pl.when(n == 2)(lambda: run_2(0))
        pl.when(n == 5)(lambda: run_2(1))
        source = keys_of(lax.select(n == 0, 0, order(n)))
        for i, total in enumerate(attend(source, range(8))):
            totals[i] = total
        return _

    lax.fori_loop(0, 7, use_source, 0)
    source = keys_of(order(7))

    def o_copy(i, off):
        return remote(osend.at[i], att.at[chip], (d, 2 * i + core), o_send.at[off], o_recv.at[off])

    for offs in ((6, 7, 4, 5), (2, 3, 1, 0)):
        tiles = [flip(chip, off) for off in offs]
        for off, i, total in zip(offs, tiles, attend(source, tiles, last=True)):
            osend[i] = (total[0:96] / total[96:97]).astype(BF16)
            if off:
                o_copy(i, off).start()
    o_keep = pltpu.make_async_copy(osend.at[chip], att.at[chip], load_sem.at[7])
    o_keep.start()

    run_3(0)
    loads[2].wait()
    o_keep.wait()
    for off in range(1, 8):
        slot = att.at[flip(chip, off)]
        remote(slot, slot, peer(off), o_send.at[off], o_recv.at[off]).wait_recv()
    normed[:, 0:768] = jnp.transpose(att[...].reshape(768, HERE))

    def add_out(i):
        cols = slice(512 * i, 512 * i + 512)
        resid[:, cols] = xv[:, cols].astype(F32) + jnp.dot(
            normed[:, 0:768], wo[:, cols], preferred_element_type=F32
        )

    for i in range(3):
        add_out(i)
    run_3(1)

    small[2].wait()

    def norm_residual(i, _):
        rows = pl.ds(pl.multiple_of(256 * i, 256), 256)
        normed[rows, :] = norm(resid[rows, :], conv_gain[...]).astype(BF16)
        return _

    lax.fori_loop(0, HERE // 256, norm_residual, 0)

    def edge_copies(n, v):
        cols = pl.ds(pl.multiple_of(SHARD * v, 128), SHARD)
        return [
            remote(ext.at[pl.ds(256, 16), cols], ext.at[pl.ds(0, 16), cols], right, h_send.at[0, n], h_recv.at[0, n]),
            remote(ext.at[pl.ds(16, 16), cols], ext.at[pl.ds(272, 16), cols], left, h_send.at[1, n], h_recv.at[1, n]),
        ]

    edges = []

    def gate(n, v):
        cols = pl.ds(pl.multiple_of(SHARD * v, 128), SHARD)
        both = pl.ds(pl.multiple_of(2 * SHARD * v, 256), 2 * SHARD)
        wide = jnp.dot(normed[...], cw[:, both], preferred_element_type=F32)
        ext[16:272, cols] = (wide[:, :SHARD] * jax.nn.sigmoid(wide[:, SHARD:])).astype(BF16)
        for copy in edge_copies(n, v):
            copy.start()
            edges.append(copy)

    here_0, here_1 = ids[0, 2 * c], ids[0, 2 * c + 1]
    before = ids[0, lax.max(2 * c - 1, 0)]
    after = ids[0, lax.min(2 * c + 2, BLOCKS - 1)]
    inner = here_0 == here_1
    keeps = (
        (jnp.logical_and(c > 0, before == here_0), inner),
        (inner, jnp.logical_and(c < 15, after == here_1)),
    )

    def taps(n, v):
        for copy in edge_copies(n, v):
            copy.wait_recv()

        def filter_lanes(i, _):
            cols = pl.ds(pl.multiple_of(SHARD * v + BLOCK * i, BLOCK), BLOCK)
            for t in range(2):
                head = ext[BLOCK * t : BLOCK * t + 16, cols].astype(F32)
                tail = ext[BLOCK * t + 144 : BLOCK * t + 160, cols].astype(F32)
                tmp[t, 0:16, :] = jnp.where(keeps[t][0], head, 0.0)
                tmp[t, 16:144, :] = ext[BLOCK * t + 16 : BLOCK * t + 144, cols].astype(F32)
                tmp[t, 144:160, :] = jnp.where(keeps[t][1], tail, 0.0)
                total = jnp.zeros((BLOCK, BLOCK), F32)
                for tap in range(KERNEL):
                    total += dw[tap : tap + 1, cols] * tmp[t, tap + 1 : tap + 1 + BLOCK, :]
                filt[BLOCK * t : BLOCK * t + BLOCK, cols] = total
            return _

        for i in range(3):
            filter_lanes(i, 0)

    groups = (a_up % 4, b_up % 4, d % 4, b_here % 4)
    for n in (0, 2):
        from_sibling((a_up, 0, a_down)[n], n)
    gate(0, groups[0])
    small[3].wait()
    small[4].wait()
    for n, dd in ((4, b_up), (5, b_down)):
        from_sibling(dd, n)
    gate(1, groups[1])
    run_4(0)
    loads[4].wait()
    from_sibling(a_far, 3)
    gate(2, groups[2])
    run_4(1)
    taps(0, groups[0])
    for n, dd in ((1, b_here), (6, b_far)):
        from_sibling(dd, n)
    gate(3, groups[3])
    for n in range(1, 4):
        taps(n, groups[n])

    def norm_filtered(i, _):
        rows = pl.ds(pl.multiple_of(256 * i, 256), 256)
        values = norm(filt[rows, :], depth_gain[...])
        normed[rows, :] = (values / (1.0 + jnp.exp(-values))).astype(BF16)
        return _

    lax.fori_loop(0, HERE // 256, norm_filtered, 0)

    loads[3].wait()

    def out_copy(i):
        cols = pl.ds(512 * i, 512)
        return pltpu.make_async_copy(out.at[:, cols], out_hbm.at[0, :, cols], load_sem.at[13 + i])

    def add_conv(i):
        cols = slice(512 * i, 512 * i + 512)
        out[:, cols] = (
            resid[:, cols] + jnp.dot(normed[...], co[:, cols], preferred_element_type=F32)
        ).astype(BF16)
        out_copy(i).start()

    for i in range(3):
        add_conv(i)

    gathers = [copy for p in range(2) for step in (gather_1, gather_2, gather_3, gather_4) for copy in step(p)]
    for copy in gathers + sends + edges:
        copy.wait_send()
    forward(0, skv.at[chip]).wait_send()

    def drain(off, _):
        forward(off, kv_slot(flip(chip, off), core)).wait_send()
        o_copy(flip(chip, off), off).wait_send()
        return _

    lax.fori_loop(1, 8, drain, 0)
    for i in range(3):
        out_copy(i).wait()


def local(inputs, block_ids, attn_gain, w_qkv, w_out, conv_gain, conv_in, depthwise_w, depth_gain, conv_out):
    in_hbm = pl.BlockSpec(memory_space=pl.ANY)
    dma = pltpu.SemaphoreType.DMA
    return pl.pallas_call(
        kernel,
        out_shape=jax.ShapeDtypeStruct((1, HERE, MODEL_DIM), BF16),
        in_specs=[in_hbm] * 11,
        out_specs=in_hbm,
        scratch_shapes=[
            pltpu.SMEM((1, BLOCKS), jnp.int32),
            pltpu.VMEM((MODEL_DIM,), F32),
            pltpu.VMEM((MODEL_DIM,), F32),
            pltpu.VMEM((MODEL_DIM,), F32),
            pltpu.VMEM((KERNEL, MODEL_DIM), F32),
            pltpu.VMEM((HERE, MODEL_DIM), BF16),
            pltpu.VMEM((HERE, MODEL_DIM), BF16),
            pltpu.VMEM((6, MODEL_DIM, SHARD), BF16),
            pltpu.VMEM((768, MODEL_DIM), BF16),
            pltpu.VMEM((MODEL_DIM, 2 * MODEL_DIM), BF16),
            pltpu.VMEM((MODEL_DIM, MODEL_DIM), BF16),
            pltpu.VMEM((LONG, 2, HALF, BLOCK), F32),
            pltpu.VMEM((HERE, MODEL_DIM), BF16),
            pltpu.VMEM((8, HEAD_DIM, HERE), BF16),
            pltpu.VMEM((8, 2, HEAD_DIM, HERE), BF16),
            pltpu.VMEM((8, BLOCK, HERE), BF16),
            pltpu.VMEM((8, 2, BLOCK, 2 * HERE), BF16),
            pltpu.VMEM((2 * HERE, BLOCK), BF16),
            pltpu.VMEM((8, 1, HERE), F32),
            pltpu.VMEM((8, 112, HERE), F32),
            pltpu.VMEM((8, HEAD_DIM, HERE), BF16),
            pltpu.VMEM((8, HEAD_DIM, HERE), BF16),
            pltpu.VMEM((HERE, MODEL_DIM), F32),
            pltpu.VMEM((HERE, MODEL_DIM), F32),
            pltpu.VMEM((HERE + 32, MODEL_DIM), BF16),
            pltpu.VMEM((2, 160, BLOCK), F32),
            dma((16,)), dma((6,)), dma((8,)), dma((8,)), dma((8,)), dma((8,)), dma((8,)), dma((8,)), dma((8,)), dma((8,)),
            dma((2, 9)), dma((2, 9)), dma((2, 7)), dma((2, 7)), dma((2, 4)), dma((2, 4)),
        ],
        compiler_params=pltpu.CompilerParams(
            collective_id=0, has_side_effects=True, vmem_limit_bytes=56 * 1024 * 1024
        ),
        name="conformer",
    )(
        inputs, block_ids, attn_gain, w_qkv, w_out, conv_gain, conv_in, depthwise_w,
        depth_gain, conv_out, jnp.asarray(rotation_tables()),
    )


def solution(mesh):
    return jax.shard_map(
        local,
        mesh=mesh,
        in_specs=(
            P("dp", "ctx", None),
            P("dp", None),
            P(),
            P(),
            P(),
            P(),
            P(None, "dp"),
            P(),
            P(),
            P(),
        ),
        out_specs=P("dp", "ctx", None),
        check_vma=False,
    )
```
